512 devices in a mesh: tm: 32 (over z, core), obs: 16 (over y, x).
Axes of the slice: x: 4, y: 4, z: 16, core: 2. Of those that a mesh axis runs over, the one named last changes fastest.
Arguments:
- footprints: bfloat16 [512, 4, 128, 128], P(('tm', 'obs')), may hold values from -0.5 to 0.5
- block_times: int32 [512, 4], P(('tm', 'obs')), may hold values from 0 to 7
- block_cells: int32 [512, 4], P(('tm', 'obs')), may hold values from 0 to 511
- live_counts: int32 [512], P(('tm', 'obs')), may hold values from 1 to 4
- cell_lat: int32 [65536], replicated, may hold values from 0 to 179
- cell_lon: int32 [65536], replicated, may hold values from 0 to 359
Outputs:
- cross_cov: float32 [65536, 4096], P(('tm', 'obs'))
- footprint_cov: float32 [512, 4, 128, 128], P(('tm', 'obs'))
The draws below stay inside these ranges and needn't reach their ends.
All inputs are finite; a program needn't handle non-finite values.
Results may differ from the reference program's by a relative error of at most 0.004.
Values may be sent and summed in bfloat16 or wider, within the bound.
No kernel may reach another device: no remote copies, remote signals or barrier semaphores. Data moves between devices by JAX's collectives and lax.ppermute only.
A program may use at most 64 MiB of HBM per device.

```python
import math
import jax
import jax.numpy as jnp
from jax import lax

BLOCK = 128
NCB = 512
SLOTS = 4
BLOCKS_DEV = 1
TSTEP = 8
NCELL = 65536
BLOCKS = 512
N_TM = 32
N_OBS = 16


def with_ends(array, stream_key, smallest, high):
    extent = array.shape
    spot = [jax.random.randint(jax.random.fold_in(stream_key, axis), (), 0, extent[axis]) for axis in range(len(extent))]
    array = array.at[tuple(spot)].set(smallest)
    longest = extent.index(max(extent))
    spot[longest] = (spot[longest] + 1) % extent[longest]
    return array.at[tuple(spot)].set(high)


def level_of(rng, extent, pieces, smallest, high):
    level = 1.0
    for dim, shards_of in pieces:
        steps = jax.random.uniform(jax.random.fold_in(jax.random.fold_in(rng, 6), dim), (shards_of,), jnp.float32, smallest / len(pieces), high / len(pieces))
        level = level * jnp.repeat(jnp.exp(steps), extent[dim] // shards_of).reshape((-1,) + (1,) * (len(extent) - 1 - dim))
    return level


def noise(own_key, shape, deviation, limit, split=(), dtype=jnp.bfloat16):
    result = jax.random.normal(own_key, shape, jnp.float32) * deviation
    if len(split) > 0:
        result = level_of(own_key, shape, split, -0.22, 0.18) * result
    return jnp.clip(result, min=-limit, max=limit).astype(dtype)


def setup_inputs(seed: int = 0) -> dict:
    key_list = jax.random.split(jax.random.key(seed), 7)
    footprints = noise(key_list[0], (BLOCKS, SLOTS, BLOCK, BLOCK), BLOCK ** -0.5, 0.5, ((0, 512),))
    block_times = with_ends(jax.random.randint(key_list[1], (BLOCKS, SLOTS), 0, TSTEP), jax.random.fold_in(key_list[1], 1), 0, TSTEP - 1).astype(jnp.int32)
    block_cells = with_ends(jax.random.randint(key_list[2], (BLOCKS, SLOTS), 0, NCB), jax.random.fold_in(key_list[2], 1), 0, NCB - 1).astype(jnp.int32)
    live_counts = with_ends(jax.random.randint(key_list[3], (BLOCKS,), 1, SLOTS + 1), jax.random.fold_in(key_list[3], 1), 1, SLOTS).astype(jnp.int32)
    cell_lat = with_ends(jax.random.randint(key_list[4], (NCELL,), 0, 180), jax.random.fold_in(key_list[4], 1), 0, 179).astype(jnp.int32)
    cell_lon = with_ends(jax.random.randint(key_list[5], (NCELL,), 0, 360), jax.random.fold_in(key_list[5], 1), 0, 359).astype(jnp.int32)
    return dict(footprints=footprints, block_times=block_times, block_cells=block_cells, live_counts=live_counts, cell_lat=cell_lat, cell_lon=cell_lon)


corr_length = 0.6

def unit_vectors(cell_lat, cell_lon):
    radians = math.pi / 180.0
    latitude = (cell_lat.astype(jnp.float32) - 89.5) * radians
    longitude = (cell_lon.astype(jnp.float32) + 0.5) * radians
    return jnp.stack([jnp.cos(latitude) * jnp.cos(longitude), jnp.cos(latitude) * jnp.sin(longitude), jnp.sin(latitude)])

def kernel_weights(own_vec, own_time, far_vec, far_time, steps):
    squared = jnp.zeros((), jnp.float32)
    for component in range(3):
        offset = own_vec[:, :, None, component, :, None] - far_vec[None, None, :, component, None, :]
        squared = squared + offset * offset
    spatial = jnp.exp(-jnp.sqrt(squared) / corr_length)
    lagged = jnp.abs(own_time[:, :, None] - far_time[None, None, :])
    temporal = jnp.exp(-lagged / steps)
    weights = (temporal[:, :, :, None, None] * spatial).astype(jnp.bfloat16)
    own_count, own_slots, far_slots, edge, _ = weights.shape
    return weights.transpose(0, 1, 3, 2, 4).reshape(own_count, own_slots * edge, far_slots * edge)

def reference(footprints, block_times, block_cells, live_counts, cell_lat, cell_lon):
    per_time = BLOCKS_DEV * N_OBS
    total = BLOCKS_DEV * N_OBS * N_TM
    steps = float(TSTEP)
    slot_live = jnp.arange(SLOTS)[None, :] < live_counts[:, None]
    prints = jnp.where(slot_live[:, :, None, None], footprints, jnp.zeros((), jnp.bfloat16))
    vectors = unit_vectors(cell_lat, cell_lon).reshape(3, NCB, BLOCK).transpose(1, 0, 2)
    block_index = jnp.arange(total).astype(jnp.int32)
    global_time = (block_index // per_time * TSTEP)[:, None] + block_times
    global_time = global_time.astype(jnp.float32)
    cats = prints.transpose(0, 2, 1, 3).reshape(total, BLOCK, SLOTS * BLOCK)
    cell_vec = vectors[block_cells]

    def one_row(index):
        own_cat = cats[index][None].astype(jnp.float32)
        own_vec = cell_vec[index][None]
        own_time = global_time[index][None]
        first = index // per_time * per_time - per_time

        def column(offset):
            far = first + offset
            valid = far >= 0
            safe = jnp.maximum(far, 0).astype(jnp.int32)
            weights = kernel_weights(own_vec, own_time, cell_vec[safe], global_time[safe], steps)
            gain = jnp.einsum('sac,scd->sad', own_cat, weights.astype(jnp.float32))[0]
            far_cat = jnp.where(valid, cats[safe], jnp.zeros((), jnp.bfloat16))
            return jnp.dot(gain.astype(jnp.bfloat16), far_cat.T, preferred_element_type=jnp.float32)
        tiles = jax.vmap(column)(jnp.arange(2 * per_time).astype(jnp.int32))
        self_weights = kernel_weights(own_vec, own_time, own_vec[0], own_time[0], steps)
        self_gain = jnp.einsum('sac,scd->sad', own_cat, self_weights.astype(jnp.float32))[0]
        covered = self_gain.reshape(BLOCK, SLOTS, BLOCK).transpose(1, 0, 2)
        return (tiles, covered)
    tiles, footprint_cov = lax.map(one_row, block_index)
    cross_cov = tiles.transpose(0, 2, 1, 3).reshape(total * BLOCK, 2 * per_time * BLOCK)
    return (cross_cov, footprint_cov)
```

```python
import functools
import math

import jax
import jax.numpy as jnp
from jax import lax
from jax.experimental import pallas as pl
from jax.experimental.pallas import tpu as pltpu
from jax.sharding import PartitionSpec as P

BLOCK = 128
SLOTS = 4
WIDE = SLOTS * BLOCK
TSTEP = 8
CORR = 0.6
DEPTH = 32
LOG2E = math.log2(math.e)
SCALE = (LOG2E / CORR) ** 2
DECAY = LOG2E / TSTEP
TINY = 1e-12
RADIANS = math.pi / 180.0


def split3(x):
    high = x.astype(jnp.bfloat16).astype(jnp.float32)
    rest = x - high
    mid = rest.astype(jnp.bfloat16).astype(jnp.float32)
    low = (rest - mid).astype(jnp.bfloat16).astype(jnp.float32)
    return high, mid, low


def unit_rows(lat, lon):
    latitude = (lat - 89.5) * RADIANS
    longitude = (lon + 0.5) * RADIANS
    across = jnp.cos(latitude)
    return across * jnp.cos(longitude), across * jnp.sin(longitude), jnp.sin(latitude)


def far_terms(units):
    terms = []
    for unit in units:
        h, m, l = split3(unit)
        terms += [h, m, h, m, l, h]
    one = jnp.ones_like(units[0])
    return terms + [one, one, one]


def near_terms(units):
    terms = []
    for unit in units:
        h, m, l = split3(unit * (-2.0 * SCALE))
        terms += [h, h, m, m, h, l]
    return terms + list(split3(jnp.full_like(units[0], 2.0 * SCALE)))


def load_rows(meta, rows, lat_ref, lon_ref, lat_rows, lon_rows, base):
    for row in range(rows):
        for slot in range(SLOTS):
            cell = meta[row, slot]
            span = pl.ds(slot * BLOCK, BLOCK)
            lat_rows[pl.ds(base + row, 1), span] = lat_ref[pl.ds(cell, 1), :].astype(jnp.float32)
            lon_rows[pl.ds(base + row, 1), span] = lon_ref[pl.ds(cell, 1), :].astype(jnp.float32)


def prepare(far, near, n_far, n_near, lat_ref, lon_ref, lat_rows, lon_rows, far_vec, near_rows, near_vec):
    lat_rows[...] = jnp.zeros_like(lat_rows)
    lon_rows[...] = jnp.zeros_like(lon_rows)
    load_rows(far, n_far, lat_ref, lon_ref, lat_rows, lon_rows, 0)
    load_rows(near, n_near, lat_ref, lon_ref, lat_rows, lon_rows, n_far)
    units = unit_rows(lat_rows[...], lon_rows[...])
    far_vec[...] = jnp.zeros_like(far_vec)
    for q, term in enumerate(far_terms(units)):
        for row in range(n_far):
            far_vec[row, pl.ds(q, 1), :] = term[row : row + 1]
    near_rows[...] = jnp.zeros_like(near_rows)
    for q, term in enumerate(near_terms(units)):
        for row in range(n_near):
            near_rows[row, pl.ds(q, 1), :] = term[n_far + row : n_far + row + 1]
    for row in range(n_near):
        near_vec[row] = near_rows[row].T.astype(jnp.bfloat16)


def one_gain(far, near, r, s, cat, far_block, near_vec, weights):
    times = jnp.concatenate(
        [jnp.full((1, BLOCK), far[r, SLOTS + j], jnp.int32) for j in range(SLOTS)], axis=1
    ).astype(jnp.float32)
    for k in range(SLOTS):
        rows = pl.ds(k * BLOCK, BLOCK)
        own_time = near[s, SLOTS + k].astype(jnp.float32)
        lag = jnp.abs(own_time - times) * (-DECAY)
        square = jnp.maximum(
            jnp.dot(near_vec[s, rows, :], far_block, preferred_element_type=jnp.float32), TINY
        )
        weights[rows, :] = jnp.exp2(lag - square * lax.rsqrt(square)).astype(jnp.bfloat16)
    return jnp.dot(cat, weights[...], preferred_element_type=jnp.float32)


def gains_kernel(n_far, far, near, lat_ref, lon_ref, cats, out, lat_rows, lon_rows, far_vec, near_rows, near_vec, weights):
    r = pl.program_id(0)

    @pl.when(r == 0)
    def _():
        prepare(far, near, n_far, 2, lat_ref, lon_ref, lat_rows, lon_rows, far_vec, near_rows, near_vec)

    far_block = far_vec[r].astype(jnp.bfloat16)
    for s in range(2):
        gain = one_gain(far, near, r, s, cats[s], far_block, near_vec, weights)
        out[s, 0] = gain.astype(jnp.bfloat16)


def self_kernel(near, lat_ref, lon_ref, cat, out, lat_rows, lon_rows, far_vec, near_rows, near_vec, weights):
    prepare(near, near, 1, 1, lat_ref, lon_ref, lat_rows, lon_rows, far_vec, near_rows, near_vec)
    gain = one_gain(near, near, 0, 0, cat[0], far_vec[0].astype(jnp.bfloat16), near_vec, weights)
    for j in range(SLOTS):
        out[0, j] = gain[:, j * BLOCK : (j + 1) * BLOCK]


def scratch_of(n_far, n_near):
    rows = -(-(n_far + n_near) // 8) * 8
    return [
        pltpu.VMEM((rows, WIDE), jnp.float32),
        pltpu.VMEM((rows, WIDE), jnp.float32),
        pltpu.VMEM((n_far, DEPTH, WIDE), jnp.float32),
        pltpu.VMEM((n_near, DEPTH, WIDE), jnp.float32),
        pltpu.VMEM((n_near, WIDE, DEPTH), jnp.bfloat16),
        pltpu.VMEM((WIDE, WIDE), jnp.bfloat16),
    ]


def whole(*shape):
    return pl.BlockSpec(shape, lambda *_: (0,) * len(shape))


def self_gain(near, lat, lon, cat):
    return pl.pallas_call(
        self_kernel,
        out_shape=jax.ShapeDtypeStruct((1, SLOTS, BLOCK, BLOCK), jnp.float32),
        in_specs=[pl.BlockSpec(memory_space=pltpu.SMEM)] + [pl.BlockSpec(memory_space=pltpu.VMEM)] * 3,
        out_specs=pl.BlockSpec(memory_space=pltpu.VMEM),
        scratch_shapes=scratch_of(1, 1),
        compiler_params=pltpu.CompilerParams(vmem_limit_bytes=24 * 2**20),
        cost_estimate=pl.CostEstimate(flops=10**8, bytes_accessed=10**6, transcendentals=2**19),
        name="self_gain",
    )(near, lat, lon, cat)


def gains(far, near, lat, lon, cats):
    n_far = far.shape[0]
    return pl.pallas_call(
        functools.partial(gains_kernel, n_far),
        grid=(n_far,),
        out_shape=jax.ShapeDtypeStruct((2, n_far, BLOCK, WIDE), jnp.bfloat16),
        in_specs=[pl.BlockSpec(memory_space=pltpu.SMEM)] * 2
        + [whole(*lat.shape), whole(*lon.shape), whole(*cats.shape)],
        out_specs=pl.BlockSpec((2, 1, BLOCK, WIDE), lambda r: (0, r, 0, 0)),
        scratch_shapes=scratch_of(n_far, 2),
        compiler_params=pltpu.CompilerParams(vmem_limit_bytes=32 * 2**20),
        cost_estimate=pl.CostEstimate(flops=3 * 10**9, bytes_accessed=8 * 10**6, transcendentals=2**24),
        name="gains",
    )(far, near, lat, lon, cats)


def tiles_kernel(group, gain, cat, out):
    for i in range(group):
        tile = lax.dot_general(
            gain[0, i], cat[i], (((1,), (1,)), ((), ())), preferred_element_type=jnp.float32
        )
        out[:, i * BLOCK : (i + 1) * BLOCK] = tile.astype(out.dtype)


def tiles(gain, cats, which, dtype, blocks, shift):
    n_far = cats.shape[0]
    group = 4
    return pl.pallas_call(
        functools.partial(tiles_kernel, group),
        grid=(n_far // group,),
        out_shape=jax.ShapeDtypeStruct((BLOCK, blocks * BLOCK), dtype),
        in_specs=[
            pl.BlockSpec((1, group, BLOCK, WIDE), lambda i: (which, i, 0, 0)),
            pl.BlockSpec((group, BLOCK, WIDE), lambda i: (i, 0, 0)),
        ],
        out_specs=pl.BlockSpec((BLOCK, group * BLOCK), lambda i: (0, i + shift // group)),
        compiler_params=pltpu.CompilerParams(vmem_limit_bytes=24 * 2**20),
        cost_estimate=pl.CostEstimate(flops=3 * 10**8, bytes_accessed=5 * 10**6, transcendentals=0),
        name="tiles",
    )(gain, cats)


def widen_kernel(tile, whole_ref, out):
    del whole_ref
    out[...] = tile[...].astype(jnp.float32)


def put_earlier(tile, cross):
    steps = 2
    width = tile.shape[1] // steps
    return pl.pallas_call(
        widen_kernel,
        grid=(steps,),
        out_shape=jax.ShapeDtypeStruct(cross.shape, cross.dtype),
        in_specs=[
            pl.BlockSpec((BLOCK, width), lambda i: (0, i)),
            pl.BlockSpec(memory_space=pl.ANY),
        ],
        out_specs=pl.BlockSpec((BLOCK, width), lambda i: (0, i)),
        input_output_aliases={1: 0},
        compiler_params=pltpu.CompilerParams(vmem_limit_bytes=24 * 2**20),
        name="put_earlier",
    )(tile, cross)


def on_device(footprints, block_times, block_cells, live_counts, cell_lat, cell_lon):
    group = lax.axis_size("obs")
    spans = lax.axis_size("tm")
    forward = [(i, i + 1) for i in range(spans - 1)]
    backward = [(i + 1, i) for i in range(spans - 1)]
    time_index = lax.axis_index("tm")
    lat = cell_lat.reshape(-1, BLOCK)
    lon = cell_lon.reshape(-1, BLOCK)
    slot_live = jnp.arange(SLOTS)[None, :] < live_counts[:, None]
    prints = jnp.where(slot_live[:, :, None, None], footprints, jnp.zeros((), jnp.bfloat16))
    cat = prints.transpose(0, 2, 1, 3).reshape(1, BLOCK, WIDE)
    pattern = jnp.concatenate([block_cells, time_index * TSTEP + block_times], axis=1)

    far = lax.all_to_all(jnp.broadcast_to(pattern, (group, 2 * SLOTS)), "obs", 0, 0, tiled=True)
    far_cats = lax.all_to_all(jnp.broadcast_to(cat, (group, BLOCK, WIDE)), "obs", 0, 0, tiled=True)
    next_cat = lax.ppermute(cat, "tm", backward)
    next_pattern = lax.ppermute(pattern, "tm", backward)

    footprint_cov = self_gain(pattern, lat, lon, cat)
    near = jnp.concatenate([pattern, next_pattern], axis=0)
    gain = gains(far, near, lat, lon, jnp.concatenate([cat, next_cat], axis=0))
    onward = tiles(gain, far_cats, 1, jnp.bfloat16, group, 0)
    earlier = lax.ppermute(onward, "tm", forward)
    cross = tiles(gain, far_cats, 0, jnp.float32, 2 * group, group)
    cross_cov = put_earlier(earlier, cross)
    return (cross_cov, footprint_cov)


def solution(mesh):
    placed = (
        P(("tm", "obs"), None, None, None),
        P(("tm", "obs"), None),
        P(("tm", "obs"), None),
        P(("tm", "obs")),
        P(),
        P(),
    )
    return jax.shard_map(
        on_device,
        mesh=mesh,
        in_specs=placed,
        out_specs=(P(("tm", "obs"), None), P(("tm", "obs"), None, None, None)),
        check_vma=False,
    )
```

```python
import functools
import math

import jax
import jax.numpy as jnp
from jax import lax
from jax.experimental import pallas as pl
from jax.experimental.pallas import tpu as pltpu
from jax.sharding import PartitionSpec as P

BLOCK = 128
SLOTS = 4
WIDE = SLOTS * BLOCK
PATTERN = 16
ROWS = BLOCK + PATTERN
PARTS = 3
DEPTH = PARTS * PATTERN
ONE_ROW = 9
TIME_ROW = 10
TSTEP = 8
CORR = 0.6
SCALE = (math.log2(math.e) / CORR) ** 2
DECAY = math.log2(math.e) / TSTEP
TINY = 1e-12
RADIANS = math.pi / 180.0
SIDE = 4
PAIR = 2


def rounded(x):
    return x.astype(jnp.bfloat16).astype(jnp.float32)


def split3(x):
    high = rounded(x)
    mid = rounded(x - high)
    return high, mid, rounded(x - high - mid)


def block_kernel(count, prints, times, cells, live, lat_ref, lon_ref, block, payload, lat_row, lon_row, pattern, sems):
    copies = []
    for j in range(SLOTS):
        for source, target, sem in ((lat_ref, lat_row, 0), (lon_ref, lon_row, 1)):
            copy = pltpu.make_async_copy(source.at[cells[0, j]], target.at[j], sems.at[sem, j])
            copy.start()
            copies.append(copy)
    for j in range(SLOTS):
        kept = jnp.where(j < live[0], prints[0, j], jnp.zeros((BLOCK, BLOCK), jnp.bfloat16))
        block[0, 0:BLOCK, j * BLOCK : (j + 1) * BLOCK] = kept
    base = lax.axis_index("tm") * TSTEP
    for copy in copies:
        copy.wait()
    lat = jnp.concatenate([lat_row[j] for j in range(SLOTS)], axis=1).astype(jnp.float32)
    lon = jnp.concatenate([lon_row[j] for j in range(SLOTS)], axis=1).astype(jnp.float32)
    latitude = (lat - 89.5) * RADIANS
    longitude = (lon + 0.5) * RADIANS
    across = jnp.cos(latitude)
    units = (across * jnp.cos(longitude), across * jnp.sin(longitude), jnp.sin(latitude))
    pattern[...] = jnp.zeros_like(pattern)
    for c, unit in enumerate(units):
        for part, value in enumerate(split3(unit)):
            pattern[pl.ds(PARTS * c + part, 1), :] = value
    pattern[pl.ds(ONE_ROW, 1), :] = jnp.ones((1, WIDE), jnp.float32)
    for j in range(SLOTS):
        when = (base + times[0, j]).astype(jnp.float32)
        pattern[pl.ds(TIME_ROW, 1), j * BLOCK : (j + 1) * BLOCK] = jnp.full((1, BLOCK), when)
    block[0, BLOCK:ROWS, :] = pattern[...].astype(jnp.bfloat16)
    for i in range(count):
        payload[i] = block[0]


def make_block(footprints, times, cells, live, lat, lon, count):
    smem = pl.BlockSpec(memory_space=pltpu.SMEM)
    vmem = pl.BlockSpec(memory_space=pltpu.VMEM)
    hbm = pl.BlockSpec(memory_space=pl.ANY)
    return pl.pallas_call(
        functools.partial(block_kernel, count),
        out_shape=(
            jax.ShapeDtypeStruct((1, ROWS, WIDE), jnp.bfloat16),
            jax.ShapeDtypeStruct((count, ROWS, WIDE), jnp.bfloat16),
        ),
        in_specs=[vmem, smem, smem, smem, hbm, hbm],
        out_specs=(vmem, vmem),
        scratch_shapes=[
            pltpu.VMEM((SLOTS, 1, BLOCK), jnp.int32),
            pltpu.VMEM((SLOTS, 1, BLOCK), jnp.int32),
            pltpu.VMEM((PATTERN, WIDE), jnp.float32),
            pltpu.SemaphoreType.DMA((2, SLOTS)),
        ],
        compiler_params=pltpu.CompilerParams(vmem_limit_bytes=12 * 2**20),
        name="make_block",
    )(footprints, times, cells, live, lat, lon)


def prepare_near(block, near_rows):
    pattern = block[0, BLOCK:ROWS, :].astype(jnp.float32)
    near_rows[...] = jnp.zeros_like(near_rows)
    for c in range(3):
        high, mid, low = (pattern[PARTS * c + part : PARTS * c + part + 1] for part in range(PARTS))
        scaled = split3((high + mid + low) * (-2.0 * SCALE))
        for segment, value in enumerate(scaled):
            for part in range(PARTS - segment):
                near_rows[pl.ds(segment * PATTERN + PARTS * c + part, 1), :] = value
    ends = split3(jnp.full((1, WIDE), 2.0 * SCALE, jnp.float32))
    for segment, value in enumerate(ends):
        near_rows[pl.ds(segment * PATTERN + ONE_ROW, 1), :] = value
    near_rows[pl.ds(TIME_ROW, 1), :] = jnp.zeros((1, WIDE), jnp.float32)
    return near_rows[...].T.astype(jnp.bfloat16), pattern[TIME_ROW : TIME_ROW + 1]


def weigh(near_vec, near_time, far_pattern, weights):
    far_vec = jnp.concatenate([far_pattern] * PARTS, axis=0)
    far_time = far_pattern.astype(jnp.float32)[TIME_ROW : TIME_ROW + 1]
    for k in range(SLOTS):
        rows = pl.ds(k * BLOCK, BLOCK)
        own = jnp.concatenate([near_time[:, k * BLOCK : (k + 1) * BLOCK]] * SLOTS, axis=1)
        lag = jnp.abs(own - far_time) * (-DECAY)
        square = jnp.maximum(jnp.dot(near_vec[rows, :], far_vec, preferred_element_type=jnp.float32), TINY)
        weights[rows, :] = jnp.exp2(lag - square * lax.rsqrt(square)).astype(jnp.bfloat16)


def self_kernel(block, out, near_rows, near_vec, weights):
    near_vec[...], when = prepare_near(block, near_rows)
    weigh(near_vec, when, block[0, BLOCK:ROWS, :], weights)
    gain = jnp.dot(block[0, 0:BLOCK, :], weights[...], preferred_element_type=jnp.float32)
    for j in range(SLOTS):
        out[0, j] = gain[:, j * BLOCK : (j + 1) * BLOCK]


def self_gain(block):
    return pl.pallas_call(
        self_kernel,
        out_shape=jax.ShapeDtypeStruct((1, SLOTS, BLOCK, BLOCK), jnp.float32),
        in_specs=[pl.BlockSpec(memory_space=pltpu.VMEM)],
        out_specs=pl.BlockSpec(memory_space=pltpu.VMEM),
        scratch_shapes=[
            pltpu.VMEM((DEPTH, WIDE), jnp.float32),
            pltpu.VMEM((WIDE, DEPTH), jnp.bfloat16),
            pltpu.VMEM((WIDE, WIDE), jnp.bfloat16),
        ],
        compiler_params=pltpu.CompilerParams(vmem_limit_bytes=12 * 2**20),
        cost_estimate=pl.CostEstimate(flops=2 * 10**9, bytes_accessed=10**6, transcendentals=2**19),
        name="self_gain",
    )(block)


def tiles_kernel(count, *refs):
    blocks, far, outs = refs[:count], refs[count], refs[count + 1 : 2 * count + 1]
    near_rows, near_vec, near_time, cats, tiles, weights = refs[2 * count + 1 :]
    n_far = far.shape[0]
    units = count * n_far
    for s in range(count):
        vec, when = prepare_near(blocks[s], near_rows)
        near_vec[s] = vec
        near_time[s] = jnp.broadcast_to(when, near_time.shape[1:])
        cats[s] = blocks[s][0, 0:BLOCK, :]

    def weigh_unit(u, slot):
        s, r = u // n_far, lax.rem(u, n_far)
        weigh(near_vec.at[s], near_time[s, 0:1, :], far[r, BLOCK:ROWS, :], weights.at[slot])

    def tile_unit(u, slot):
        s, r = u // n_far, lax.rem(u, n_far)
        gain = jnp.dot(cats[s], weights[slot], preferred_element_type=jnp.float32)
        tiles[u] = lax.dot_general(
            gain.astype(jnp.bfloat16),
            far[r, 0:BLOCK, :],
            (((1,), (1,)), ((), ())),
            preferred_element_type=jnp.float32,
        ).astype(tiles.dtype)

    def turn(i, carry):
        u = 2 * i
        weigh_unit(u, 0)
        tile_unit(jnp.maximum(u - 1, 0), 1)
        weigh_unit(u + 1, 1)
        tile_unit(u, 0)
        return carry

    lax.fori_loop(0, units // 2, turn, 0)
    tile_unit(units - 1, 1)
    for u in range(units):
        s, r = u // n_far, u % n_far
        outs[s][:, r * BLOCK : (r + 1) * BLOCK] = tiles[u]


def make_tiles(blocks, far, dtype):
    count, n_far = len(blocks), far.shape[0]
    vmem = pl.BlockSpec(memory_space=pltpu.VMEM)
    shape = jax.ShapeDtypeStruct((BLOCK, n_far * BLOCK), dtype)
    return pl.pallas_call(
        functools.partial(tiles_kernel, count),
        out_shape=(shape,) * count,
        in_specs=[vmem] * (count + 1),
        out_specs=(vmem,) * count,
        scratch_shapes=[
            pltpu.VMEM((DEPTH, WIDE), jnp.float32),
            pltpu.VMEM((count, WIDE, DEPTH), jnp.bfloat16),
            pltpu.VMEM((count, 8, WIDE), jnp.float32),
            pltpu.VMEM((count, BLOCK, WIDE), jnp.bfloat16),
            pltpu.VMEM((count * n_far, BLOCK, BLOCK), dtype),
            pltpu.VMEM((2, WIDE, WIDE), jnp.bfloat16),
        ],
        compiler_params=pltpu.CompilerParams(vmem_limit_bytes=16 * 2**20),
        cost_estimate=pl.CostEstimate(
            flops=count * 10**9, bytes_accessed=count * 2 * 10**6, transcendentals=count * 2**22
        ),
        name="make_tiles",
    )(*blocks, far)


def place_kernel(own, partner, before, before_partner, out):
    step = pl.program_id(0)
    lower = lax.rem(lax.axis_index("obs"), SIDE) < PAIR
    half = PAIR * BLOCK
    mine = jnp.where(step < SIDE, before[...].astype(jnp.float32), own[...])
    other = jnp.where(step < SIDE, before_partner[...], partner[...]).astype(jnp.float32)
    out[:, 0:half] = jnp.where(lower, mine, other)
    out[:, half:] = jnp.where(lower, other, mine)


def place(own, partner, before, before_partner):
    half = PAIR * BLOCK
    late = pl.BlockSpec((BLOCK, half), lambda i: (0, jnp.maximum(i - SIDE, 0)))
    early = pl.BlockSpec((BLOCK, half), lambda i: (0, jnp.minimum(i, SIDE - 1)))
    return pl.pallas_call(
        place_kernel,
        grid=(2 * SIDE,),
        out_shape=jax.ShapeDtypeStruct((BLOCK, 4 * own.shape[1]), jnp.float32),
        in_specs=[late, late, early, early],
        out_specs=pl.BlockSpec((BLOCK, 2 * half), lambda i: (0, i)),
        compiler_params=pltpu.CompilerParams(vmem_limit_bytes=12 * 2**20),
        name="place",
    )(own, partner, before, before_partner)


def on_device(footprints, block_times, block_cells, live_counts, cell_lat, cell_lon):
    group = lax.axis_size("obs")
    spans = lax.axis_size("tm")
    axes = ("tm", "obs")
    near_by = [[o for o in range(group) if o % SIDE // PAIR == b] for b in range(SIDE // PAIR)]
    across = [o // SIDE * SIDE + SIDE - 1 - o % SIDE for o in range(group)]
    to_partner = [(t * group + o, t * group + across[o]) for t in range(spans) for o in range(group)]

    def steps(by, crossing):
        return [
            (t * group + o, (t + by) * group + (across[o] if crossing else o))
            for t in range(spans)
            if 0 <= t + by < spans
            for o in range(group)
        ]

    lat = cell_lat.reshape(-1, 1, BLOCK)
    lon = cell_lon.reshape(-1, 1, BLOCK)
    block, payload = make_block(
        footprints, block_times, block_cells, live_counts, lat, lon, group // (SIDE // PAIR)
    )
    far = lax.all_to_all(payload, "obs", 0, 0, tiled=True, axis_index_groups=near_by)
    partner_block = lax.ppermute(block, axes, to_partner)
    next_block = lax.ppermute(block, axes, steps(-1, False))
    next_partner_block = lax.ppermute(block, axes, steps(-1, True))
    footprint_cov = self_gain(block)
    next_partner_tiles, next_tiles = make_tiles((next_partner_block, next_block), far, jnp.bfloat16)
    before_partner = lax.ppermute(next_partner_tiles, axes, steps(1, True))
    before = lax.ppermute(next_tiles, axes, steps(1, False))
    (partner_tiles,) = make_tiles((partner_block,), far, jnp.bfloat16)
    partner = lax.ppermute(partner_tiles, axes, to_partner)
    (own,) = make_tiles((block,), far, jnp.float32)
    cross_cov = place(own, partner, before, before_partner)
    return (cross_cov, footprint_cov)


def solution(mesh):
    placed = (
        P(("tm", "obs"), None, None, None),
        P(("tm", "obs"), None),
        P(("tm", "obs"), None),
        P(("tm", "obs")),
        P(),
        P(),
    )
    return jax.shard_map(
        on_device,
        mesh=mesh,
        in_specs=placed,
        out_specs=(P(("tm", "obs"), None), P(("tm", "obs"), None, None, None)),
        check_vma=False,
    )
```

```python
import functools
import math

import jax
import jax.numpy as jnp
from jax import lax
from jax.experimental import pallas as pl
from jax.experimental.pallas import tpu as pltpu
from jax.sharding import PartitionSpec as P

BLOCK = 128
SLOTS = 4
WIDE = SLOTS * BLOCK
PATTERN = 16
ROWS = BLOCK + PATTERN
PARTS = 3
DEPTH = PARTS * PATTERN
ONE_ROW = 9
TIME_ROW = 10
LIVE_ROW = 11
CHUNK = 2 * BLOCK
TSTEP = 8
CORR = 0.6
SCALE = (math.log2(math.e) / CORR) ** 2
DECAY = math.log2(math.e) / TSTEP
TINY = 1e-12
RADIANS = math.pi / 180.0
SIDE = 4
PAIR = 2


def rounded(x):
    return x.astype(jnp.bfloat16).astype(jnp.float32)


def split3(x):
    high = rounded(x)
    mid = rounded(x - high)
    return high, mid, rounded(x - high - mid)


def block_kernel(count, prints, times, cells, live, lat_ref, lon_ref, block, payload, own, when, where, alive, lat_row, lon_row, pattern, sems, row_sems):
    loads = [
        pltpu.make_async_copy(source, target, sems.at[i])
        for i, (source, target) in enumerate(((cells, where), (times, when), (live, alive), (prints, own)))
    ]
    for load in loads:
        load.start()
    loads[0].wait()
    copies = []
    for j in range(SLOTS):
        for source, target, sem in ((lat_ref, lat_row, 0), (lon_ref, lon_row, 1)):
            copy = pltpu.make_async_copy(source.at[where[0, j]], target.at[j], row_sems.at[sem, j])
            copy.start()
            copies.append(copy)
    for load in loads[1:]:
        load.wait()
    for j in range(SLOTS):
        kept = jnp.where(j < alive[0], own[0, j], jnp.zeros((BLOCK, BLOCK), jnp.bfloat16))
        block[0, 0:BLOCK, j * BLOCK : (j + 1) * BLOCK] = kept
    base = lax.axis_index("tm") * TSTEP
    pattern[...] = jnp.zeros_like(pattern)
    pattern[pl.ds(ONE_ROW, 1), :] = jnp.ones((1, WIDE), jnp.float32)
    pattern[pl.ds(LIVE_ROW, 1), :] = jnp.full((1, WIDE), alive[0].astype(jnp.float32))
    for j in range(SLOTS):
        moment = (base + when[0, j]).astype(jnp.float32)
        pattern[pl.ds(TIME_ROW, 1), j * BLOCK : (j + 1) * BLOCK] = jnp.full((1, BLOCK), moment)
    for copy in copies:
        copy.wait()
    lat = jnp.concatenate([lat_row[j] for j in range(SLOTS)], axis=1).astype(jnp.float32)
    lon = jnp.concatenate([lon_row[j] for j in range(SLOTS)], axis=1).astype(jnp.float32)
    latitude = (lat - 89.5) * RADIANS
    longitude = (lon + 0.5) * RADIANS
    across = jnp.cos(latitude)
    units = (across * jnp.cos(longitude), across * jnp.sin(longitude), jnp.sin(latitude))
    for c, unit in enumerate(units):
        for part, value in enumerate(split3(unit)):
            pattern[pl.ds(PARTS * c + part, 1), :] = value
    block[0, BLOCK:ROWS, :] = pattern[...].astype(jnp.bfloat16)
    for i in range(count):
        payload[i] = block[0]


def make_block(footprints, times, cells, live, lat, lon, count):
    vmem = pl.BlockSpec(memory_space=pltpu.VMEM)
    hbm = pl.BlockSpec(memory_space=pltpu.HBM)
    return pl.pallas_call(
        functools.partial(block_kernel, count),
        out_shape=(
            jax.ShapeDtypeStruct((1, ROWS, WIDE), jnp.bfloat16),
            jax.ShapeDtypeStruct((count, ROWS, WIDE), jnp.bfloat16),
        ),
        in_specs=[hbm] * 6,
        out_specs=(vmem, vmem),
        scratch_shapes=[
            pltpu.VMEM((1, SLOTS, BLOCK, BLOCK), jnp.bfloat16),
            pltpu.SMEM((1, SLOTS), jnp.int32),
            pltpu.SMEM((1, SLOTS), jnp.int32),
            pltpu.SMEM((1,), jnp.int32),
            pltpu.VMEM((SLOTS, 1, BLOCK), jnp.int32),
            pltpu.VMEM((SLOTS, 1, BLOCK), jnp.int32),
            pltpu.VMEM((PATTERN, WIDE), jnp.float32),
            pltpu.SemaphoreType.DMA((4,)),
            pltpu.SemaphoreType.DMA((2, SLOTS)),
        ],
        compiler_params=pltpu.CompilerParams(vmem_limit_bytes=60 * 2**20),
        name="make_block",
    )(footprints, times, cells, live, lat, lon)


def prepare_near(block, near_rows):
    pattern = block[0, BLOCK:ROWS, :].astype(jnp.float32)
    near_rows[...] = jnp.zeros_like(near_rows)
    for c in range(3):
        high, mid, low = (pattern[PARTS * c + part : PARTS * c + part + 1] for part in range(PARTS))
        scaled = split3((high + mid + low) * (-2.0 * SCALE))
        for segment, value in enumerate(scaled):
            for part in range(PARTS - segment):
                near_rows[pl.ds(segment * PATTERN + PARTS * c + part, 1), :] = value
    ends = split3(jnp.full((1, WIDE), 2.0 * SCALE, jnp.float32))
    for segment, value in enumerate(ends):
        near_rows[pl.ds(segment * PATTERN + ONE_ROW, 1), :] = value
    near_rows[pl.ds(TIME_ROW, 1), :] = jnp.zeros((1, WIDE), jnp.float32)
    return near_rows[...].T.astype(jnp.bfloat16), pattern[TIME_ROW : TIME_ROW + 1]


def weigh(near_vec, near_time, far_pattern, weights, live):
    columns = far_pattern.shape[1]
    far_vec = jnp.concatenate([far_pattern] * PARTS, axis=0)
    far_time = far_pattern.astype(jnp.float32)[TIME_ROW : TIME_ROW + 1]
    for k in range(live):
        rows = pl.ds(k * BLOCK, BLOCK)
        own = jnp.concatenate([near_time[:, k * BLOCK : (k + 1) * BLOCK]] * (columns // BLOCK), axis=1)
        lag = jnp.abs(own - far_time) * (-DECAY)
        square = jnp.maximum(jnp.dot(near_vec[rows, :], far_vec, preferred_element_type=jnp.float32), TINY)
        weights[rows, :] = jnp.exp2(lag - square * lax.rsqrt(square)).astype(jnp.bfloat16)


def self_kernel(block, out, near_rows, near_vec, weights):
    near_vec[...], when = prepare_near(block, near_rows)
    weigh(near_vec, when, block[0, BLOCK:ROWS, :], weights, SLOTS)
    gain = jnp.dot(block[0, 0:BLOCK, :], weights[...], preferred_element_type=jnp.float32)
    for j in range(SLOTS):
        out[0, j] = gain[:, j * BLOCK : (j + 1) * BLOCK]


def self_gain(block):
    return pl.pallas_call(
        self_kernel,
        out_shape=jax.ShapeDtypeStruct((1, SLOTS, BLOCK, BLOCK), jnp.float32),
        in_specs=[pl.BlockSpec(memory_space=pltpu.VMEM)],
        out_specs=pl.BlockSpec(memory_space=pltpu.VMEM),
        scratch_shapes=[
            pltpu.VMEM((DEPTH, WIDE), jnp.float32),
            pltpu.VMEM((WIDE, DEPTH), jnp.bfloat16),
            pltpu.VMEM((WIDE, WIDE), jnp.bfloat16),
        ],
        compiler_params=pltpu.CompilerParams(vmem_limit_bytes=12 * 2**20),
        cost_estimate=pl.CostEstimate(flops=2 * 10**9, bytes_accessed=10**6, transcendentals=2**19),
        name="self_gain",
    )(block)


def live_of(pattern):
    count = pattern[:, 0:BLOCK].astype(jnp.float32)[LIVE_ROW : LIVE_ROW + 1]
    return jnp.max(count).astype(jnp.int32)


def columns_at(start, width):
    return pl.ds(pl.multiple_of(start, BLOCK), width)


def tiles_kernel(count, *refs):
    blocks, far, outs = refs[:count], refs[count], refs[count + 1 : 2 * count + 1]
    near_rows, near_vec, near_time, cats, far_pattern, gain, tiles, weights = refs[2 * count + 1 :]
    n_far = far.shape[0]
    near_live = []
    for s in range(count):
        vec, when = prepare_near(blocks[s], near_rows)
        near_vec[s] = vec
        near_time[s] = jnp.broadcast_to(when, near_time.shape[1:])
        cats[s] = blocks[s][0, 0:BLOCK, :]
        near_live.append(live_of(blocks[s][0, BLOCK:ROWS, :]))
    starts, filled = [], jnp.int32(0)
    for r in range(n_far):
        pattern = far[r, BLOCK:ROWS, :]
        far_pattern[:, columns_at(filled * BLOCK, WIDE)] = pattern
        starts.append(filled * BLOCK)
        filled = filled + live_of(pattern)
    far_pattern[:, columns_at(filled * BLOCK, WIDE)] = jnp.zeros((PATTERN, WIDE), jnp.bfloat16)
    turns = (filled * BLOCK + 2 * CHUNK - 1) // (2 * CHUNK)
    gain[:, columns_at(turns * 2 * CHUNK, WIDE)] = jnp.zeros((BLOCK, WIDE), jnp.bfloat16)

    def one_near(s, carry):
        live = near_live[0]
        for other in range(1, count):
            live = jnp.where(s == other, near_live[other], live)

        def weigh_chunk(start, slot, used):
            weigh(
                near_vec.at[s], near_time[s, 0:1, :], far_pattern[:, columns_at(start, CHUNK)], weights.at[slot], used
            )

        def gain_chunk(start, slot, used):
            depth = used * BLOCK
            part = jnp.dot(cats[s, :, 0:depth], weights[slot, 0:depth, :], preferred_element_type=jnp.float32)
            gain[:, columns_at(start, CHUNK)] = part.astype(jnp.bfloat16)

        for used in range(1, SLOTS + 1):

            @pl.when(live == used)
            def _(used=used):
                def turn(i, carry):
                    start = i * 2 * CHUNK
                    weigh_chunk(start, 0, used)
                    gain_chunk(jnp.maximum(start - CHUNK, 0), 1, used)
                    weigh_chunk(start + CHUNK, 1, used)
                    gain_chunk(start, 0, used)
                    return carry

                lax.fori_loop(0, turns, turn, 0)
                gain_chunk(turns * 2 * CHUNK - CHUNK, 1, used)

        for r in range(n_far):
            tiles[s * n_far + r] = lax.dot_general(
                gain[:, columns_at(starts[r], WIDE)],
                far[r, 0:BLOCK, :],
                (((1,), (1,)), ((), ())),
                preferred_element_type=jnp.float32,
            ).astype(tiles.dtype)
        return carry

    lax.fori_loop(0, count, one_near, 0)
    for u in range(count * n_far):
        s, r = u // n_far, u % n_far
        outs[s][:, r * BLOCK : (r + 1) * BLOCK] = tiles[u]


def make_tiles(blocks, far, dtype):
    count, n_far = len(blocks), far.shape[0]
    vmem = pl.BlockSpec(memory_space=pltpu.VMEM)
    shape = jax.ShapeDtypeStruct((BLOCK, n_far * BLOCK), dtype)
    return pl.pallas_call(
        functools.partial(tiles_kernel, count),
        out_shape=(shape,) * count,
        in_specs=[vmem] * (count + 1),
        out_specs=(vmem,) * count,
        scratch_shapes=[
            pltpu.VMEM((DEPTH, WIDE), jnp.float32),
            pltpu.VMEM((count, WIDE, DEPTH), jnp.bfloat16),
            pltpu.VMEM((count, 8, WIDE), jnp.float32),
            pltpu.VMEM((count, BLOCK, WIDE), jnp.bfloat16),
            pltpu.VMEM((PATTERN, (n_far + 1) * WIDE), jnp.bfloat16),
            pltpu.VMEM((BLOCK, (n_far + 1) * WIDE), jnp.bfloat16),
            pltpu.VMEM((count * n_far, BLOCK, BLOCK), dtype),
            pltpu.VMEM((2, WIDE, CHUNK), jnp.bfloat16),
        ],
        compiler_params=pltpu.CompilerParams(vmem_limit_bytes=16 * 2**20),
        cost_estimate=pl.CostEstimate(
            flops=count * 10**9, bytes_accessed=count * 2 * 10**6, transcendentals=count * 2**22
        ),
        name="make_tiles",
    )(*blocks, far)


def pair_start(x, odd):
    return jnp.where(odd, lax.rem((x + 3) // PAIR * PAIR + 1, SIDE), x // PAIR * PAIR)


def spread(source, out, base, start, sems):
    copies = []
    for y in range(SIDE):
        for i in range(PAIR):
            column = base + (y * SIDE + lax.rem(start + i, SIDE)) * BLOCK
            u = y * PAIR + i
            copies.append(
                pltpu.make_async_copy(
                    source.at[:, u * BLOCK : (u + 1) * BLOCK], out.at[:, columns_at(column, BLOCK)], sems.at[u]
                )
            )
    return copies


def place_most_kernel(own, before, before_partner, out, wide, wide_partner, sems):
    x = lax.rem(lax.axis_index("obs"), SIDE)
    odd = lax.rem(lax.axis_index("tm"), 2) == 1
    width = own.shape[1]
    earlier = pair_start(x, jnp.logical_not(odd))
    copies = spread(own, out, 2 * width, pair_start(x, odd), sems.at[0])
    for copy in copies:
        copy.start()
    wide[...] = before[...].astype(jnp.float32)
    more = spread(wide, out, 0, earlier, sems.at[1])
    for copy in more:
        copy.start()
    wide_partner[...] = before_partner[...].astype(jnp.float32)
    last = spread(wide_partner, out, 0, earlier + PAIR, sems.at[2])
    for copy in last:
        copy.start()
    for copy in copies + more + last:
        copy.wait()


def place_most(own, before, before_partner):
    vmem = pl.BlockSpec(memory_space=pltpu.VMEM)
    return pl.pallas_call(
        place_most_kernel,
        out_shape=jax.ShapeDtypeStruct((BLOCK, 4 * own.shape[1]), jnp.float32),
        in_specs=[vmem] * 3,
        out_specs=pl.BlockSpec(memory_space=pltpu.HBM),
        scratch_shapes=[
            pltpu.VMEM(own.shape, jnp.float32),
            pltpu.VMEM(own.shape, jnp.float32),
            pltpu.SemaphoreType.DMA((3, SIDE * PAIR)),
        ],
        compiler_params=pltpu.CompilerParams(vmem_limit_bytes=12 * 2**20),
        cost_estimate=pl.CostEstimate(flops=10**9, bytes_accessed=4 * 10**6, transcendentals=0),
        name="place_most",
    )(own, before, before_partner)


def place_rest_kernel(partner, filled, out, wide, sems):
    del filled
    x = lax.rem(lax.axis_index("obs"), SIDE)
    odd = lax.rem(lax.axis_index("tm"), 2) == 1
    wide[...] = partner[...].astype(jnp.float32)
    copies = spread(wide, out, 2 * wide.shape[1], pair_start(x, odd) + PAIR, sems)
    for copy in copies:
        copy.start()
    for copy in copies:
        copy.wait()


def place_rest(partner, filled):
    hbm = pl.BlockSpec(memory_space=pltpu.HBM)
    return pl.pallas_call(
        place_rest_kernel,
        out_shape=jax.ShapeDtypeStruct(filled.shape, filled.dtype),
        in_specs=[pl.BlockSpec(memory_space=pltpu.VMEM), hbm],
        out_specs=hbm,
        input_output_aliases={1: 0},
        scratch_shapes=[pltpu.VMEM(partner.shape, jnp.float32), pltpu.SemaphoreType.DMA((SIDE * PAIR,))],
        compiler_params=pltpu.CompilerParams(vmem_limit_bytes=12 * 2**20),
        name="place_rest",
    )(partner, filled)


def on_device(footprints, block_times, block_cells, live_counts, cell_lat, cell_lon):
    group = lax.axis_size("obs")
    spans = lax.axis_size("tm")
    axes = ("tm", "obs")
    sides = ((0, 1), (2, 3)), ((1, 2), (3, 0))
    near_by = [
        [t * group + y * SIDE + x for y in range(group // SIDE) for x in pair]
        for t in range(spans)
        for pair in sides[t % 2]
    ]

    def across(t, o):
        x = o % SIDE
        return o - x + (x ^ 1 if t % 2 else SIDE - 1 - x)

    def steps(by, crossing):
        pairs = []
        for t in range(spans):
            if 0 <= t + by < spans:
                for o in range(group):
                    other = across(min(t, t + by), o) if crossing else o
                    pairs.append((t * group + o, (t + by) * group + other))
        return pairs

    lat = cell_lat.reshape(-1, 1, BLOCK)
    lon = cell_lon.reshape(-1, 1, BLOCK)
    block, payload = make_block(
        footprints, block_times, block_cells, live_counts, lat, lon, group // (SIDE // PAIR)
    )
    far = lax.all_to_all(payload, axes, 0, 0, tiled=True, axis_index_groups=near_by)
    partner_block = lax.ppermute(block, axes, steps(0, True))
    next_block = lax.ppermute(block, axes, steps(-1, False))
    next_partner_block = lax.ppermute(block, axes, steps(-1, True))
    footprint_cov = self_gain(block)
    far, footprint_cov = lax.optimization_barrier((far, footprint_cov))
    (next_partner_tiles,) = make_tiles((next_partner_block,), far, jnp.bfloat16)
    before_partner = lax.ppermute(next_partner_tiles, axes, steps(1, True))
    (partner_tiles,) = make_tiles((partner_block,), far, jnp.bfloat16)
    partner = lax.ppermute(partner_tiles, axes, steps(0, True))
    (next_tiles,) = make_tiles((next_block,), far, jnp.bfloat16)
    before = lax.ppermute(next_tiles, axes, steps(1, False))
    (own,) = make_tiles((block,), far, jnp.float32)
    cross_cov = place_rest(partner, place_most(own, before, before_partner))
    return (cross_cov, footprint_cov)


def solution(mesh):
    placed = (
        P(("tm", "obs"), None, None, None),
        P(("tm", "obs"), None),
        P(("tm", "obs"), None),
        P(("tm", "obs")),
        P(),
        P(),
    )
    return jax.shard_map(
        on_device,
        mesh=mesh,
        in_specs=placed,
        out_specs=(P(("tm", "obs"), None), P(("tm", "obs"), None, None, None)),
        check_vma=False,
    )
```

```python
import functools
import math

import jax
import jax.numpy as jnp
from jax import lax
from jax.experimental import pallas as pl
from jax.experimental.pallas import tpu as pltpu
from jax.sharding import PartitionSpec as P

BLOCK = 128
SLOTS = 4
WIDE = SLOTS * BLOCK
PATTERN = 16
ROWS = BLOCK + PATTERN
PARTS = 3
DEPTH = PARTS * PATTERN
ONE_ROW = 9
TIME_ROW = 10
LIVE_ROW = 11
CHUNK = WIDE
TSTEP = 8
CORR = 0.6
SCALE = (math.log2(math.e) / CORR) ** 2
DECAY = math.log2(math.e) / TSTEP
TINY = 1e-12
RADIANS = math.pi / 180.0
SIDE = 4
PAIR = 2


def rounded(x):
    return x.astype(jnp.bfloat16).astype(jnp.float32)


def split3(x):
    high = rounded(x)
    mid = rounded(x - high)
    return high, mid, rounded(x - high - mid)


def block_kernel(
    prints, times, cells, live, lat_ref, lon_ref, block, payload, own, when, where, alive, lat, lon, cat, rows, pattern, loads_sem, sends_sem
):
    loads = [
        pltpu.make_async_copy(source, target, loads_sem.at[i])
        for i, (source, target) in enumerate(
            ((prints, own), (live, alive), (cells, where), (times, when), (lat_ref, lat), (lon_ref, lon))
        )
    ]
    for load in loads:
        load.start()
    targets = [payload.at[i] for i in range(payload.shape[0])] + [block.at[0]]

    def send(source, start, size, sem):
        copies = [
            pltpu.make_async_copy(source, target.at[pl.ds(start, size), :], sends_sem.at[sem, i])
            for i, target in enumerate(targets)
        ]
        for copy in copies:
            copy.start()
        return copies

    base = lax.axis_index("tm") * TSTEP
    loads[0].wait()
    loads[1].wait()
    for j in range(SLOTS):
        kept = jnp.where(j < alive[0], own[0, j], jnp.zeros((BLOCK, BLOCK), jnp.bfloat16))
        cat[0:BLOCK, j * BLOCK : (j + 1) * BLOCK] = kept
    sends = send(cat.at[pl.ds(0, BLOCK), :], 0, BLOCK, 0)
    for load in loads[2:]:
        load.wait()
    pattern[...] = jnp.zeros_like(pattern)
    pattern[pl.ds(ONE_ROW, 1), :] = jnp.ones((1, WIDE), jnp.float32)
    pattern[pl.ds(LIVE_ROW, 1), :] = jnp.full((1, WIDE), alive[0].astype(jnp.float32))
    for j in range(SLOTS):
        moment = (base + when[0, j]).astype(jnp.float32)
        pattern[pl.ds(TIME_ROW, 1), j * BLOCK : (j + 1) * BLOCK] = jnp.full((1, BLOCK), moment)
        rows[pl.ds(j, 1), :] = lat[pl.ds(where[0, j], 1), :]
        rows[pl.ds(SLOTS + j, 1), :] = lon[pl.ds(where[0, j], 1), :]
    degrees = rows[...].astype(jnp.float32)
    is_lat = lax.broadcasted_iota(jnp.int32, degrees.shape, 0) < SLOTS
    angles = (degrees + jnp.where(is_lat, -89.5, 0.5)) * RADIANS
    cosines, sines = jnp.cos(angles), jnp.sin(angles)
    across = cosines[0:SLOTS]
    units = (across * cosines[SLOTS:], across * sines[SLOTS:], sines[0:SLOTS])
    for c, unit in enumerate(units):
        for part, value in enumerate(split3(unit)):
            for j in range(SLOTS):
                pattern[pl.ds(PARTS * c + part, 1), j * BLOCK : (j + 1) * BLOCK] = value[j : j + 1]
    cat[BLOCK:ROWS, :] = pattern[...].astype(jnp.bfloat16)
    sends += send(cat.at[pl.ds(BLOCK, PATTERN), :], BLOCK, PATTERN, 1)
    for copy in sends:
        copy.wait()


def make_block(footprints, times, cells, live, lat, lon, count):
    hbm = pl.BlockSpec(memory_space=pltpu.HBM)
    return pl.pallas_call(
        block_kernel,
        out_shape=(
            jax.ShapeDtypeStruct((1, ROWS, WIDE), jnp.bfloat16),
            jax.ShapeDtypeStruct((count, ROWS, WIDE), jnp.bfloat16),
        ),
        in_specs=[hbm] * 6,
        out_specs=(hbm, hbm),
        scratch_shapes=[
            pltpu.VMEM((1, SLOTS, BLOCK, BLOCK), jnp.bfloat16),
            pltpu.SMEM((1, SLOTS), jnp.int32),
            pltpu.SMEM((1, SLOTS), jnp.int32),
            pltpu.SMEM((1,), jnp.int32),
            pltpu.VMEM(lat.shape, jnp.int32),
            pltpu.VMEM(lon.shape, jnp.int32),
            pltpu.VMEM((ROWS, WIDE), jnp.bfloat16),
            pltpu.VMEM((2 * SLOTS, BLOCK), jnp.int32),
            pltpu.VMEM((PATTERN, WIDE), jnp.float32),
            pltpu.SemaphoreType.DMA((6,)),
            pltpu.SemaphoreType.DMA((2, count + 1)),
        ],
        compiler_params=pltpu.CompilerParams(vmem_limit_bytes=60 * 2**20),
        name="make_block",
    )(footprints, times, cells, live, lat, lon)


def prepare_near(block, near_rows):
    pattern = block[0, BLOCK:ROWS, :].astype(jnp.float32)
    near_rows[...] = jnp.zeros_like(near_rows)
    for c in range(3):
        high, mid, low = (pattern[PARTS * c + part : PARTS * c + part + 1] for part in range(PARTS))
        scaled = split3((high + mid + low) * (-2.0 * SCALE))
        for segment, value in enumerate(scaled):
            for part in range(PARTS - segment):
                near_rows[pl.ds(segment * PATTERN + PARTS * c + part, 1), :] = value
    ends = split3(jnp.full((1, WIDE), 2.0 * SCALE, jnp.float32))
    for segment, value in enumerate(ends):
        near_rows[pl.ds(segment * PATTERN + ONE_ROW, 1), :] = value
    near_rows[pl.ds(TIME_ROW, 1), :] = jnp.zeros((1, WIDE), jnp.float32)
    return near_rows[...].T.astype(jnp.bfloat16), pattern[TIME_ROW : TIME_ROW + 1]


def weigh(near_vec, near_time, far_pattern, weights, live):
    columns = far_pattern.shape[1]
    far_vec = jnp.concatenate([far_pattern] * PARTS, axis=0)
    far_time = far_pattern.astype(jnp.float32)[TIME_ROW : TIME_ROW + 1]
    for k in range(live):
        rows = pl.ds(k * BLOCK, BLOCK)
        own = jnp.concatenate([near_time[:, k * BLOCK : (k + 1) * BLOCK]] * (columns // BLOCK), axis=1)
        lag = jnp.abs(own - far_time) * (-DECAY)
        square = jnp.maximum(jnp.dot(near_vec[rows, :], far_vec, preferred_element_type=jnp.float32), TINY)
        weights[rows, :] = jnp.exp2(lag - square * lax.rsqrt(square)).astype(jnp.bfloat16)


def self_kernel(block, out, near_rows, near_vec, weights):
    near_vec[...], when = prepare_near(block, near_rows)
    weigh(near_vec, when, block[0, BLOCK:ROWS, :], weights, SLOTS)
    gain = jnp.dot(block[0, 0:BLOCK, :], weights[...], preferred_element_type=jnp.float32)
    for j in range(SLOTS):
        out[0, j] = gain[:, j * BLOCK : (j + 1) * BLOCK]


def self_gain(block):
    return pl.pallas_call(
        self_kernel,
        out_shape=jax.ShapeDtypeStruct((1, SLOTS, BLOCK, BLOCK), jnp.float32),
        in_specs=[pl.BlockSpec(memory_space=pltpu.VMEM)],
        out_specs=pl.BlockSpec(memory_space=pltpu.VMEM),
        scratch_shapes=[
            pltpu.VMEM((DEPTH, WIDE), jnp.float32),
            pltpu.VMEM((WIDE, DEPTH), jnp.bfloat16),
            pltpu.VMEM((WIDE, WIDE), jnp.bfloat16),
        ],
        compiler_params=pltpu.CompilerParams(vmem_limit_bytes=12 * 2**20),
        cost_estimate=pl.CostEstimate(flops=2 * 10**9, bytes_accessed=10**6, transcendentals=2**19),
        name="self_gain",
    )(block)


def live_of(pattern):
    count = pattern[:, 0:BLOCK].astype(jnp.float32)[LIVE_ROW : LIVE_ROW + 1]
    return jnp.max(count).astype(jnp.int32)


def columns_at(start, width):
    return pl.ds(pl.multiple_of(start, BLOCK), width)


def tiles_kernel(count, placing, *refs):
    blocks, far = refs[:count], refs[count]
    if placing:
        before, before_partner, out = refs[count + 1 : count + 4]
        *scratch, wide, wide_partner, own, sems = refs[count + 4 :]
        outs = (own,)
        x, odd, earlier = where_placed()
        wide[...] = before[...].astype(jnp.float32)
        wide_partner[...] = before_partner[...].astype(jnp.float32)
        copies = spread(wide, out, 0, earlier, sems.at[0])
        copies += spread(wide_partner, out, 0, earlier + PAIR, sems.at[1])
        for copy in copies:
            copy.start()
    else:
        outs = refs[count + 1 : 2 * count + 1]
        scratch = refs[2 * count + 1 :]
    near_rows, near_vec, near_time, cats, far_pattern, gain, tiles, weights = scratch
    n_far = far.shape[0]
    near_live = []
    for s in range(count):
        vec, when = prepare_near(blocks[s], near_rows)
        near_vec[s] = vec
        near_time[s] = jnp.broadcast_to(when, near_time.shape[1:])
        cats[s] = blocks[s][0, 0:BLOCK, :]
        near_live.append(live_of(blocks[s][0, BLOCK:ROWS, :]))
    starts, filled = [], jnp.int32(0)
    for r in range(n_far):
        pattern = far[r, BLOCK:ROWS, :]
        far_pattern[:, columns_at(filled * BLOCK, WIDE)] = pattern
        starts.append(filled * BLOCK)
        filled = filled + live_of(pattern)
    far_pattern[:, columns_at(filled * BLOCK, WIDE)] = jnp.zeros((PATTERN, WIDE), jnp.bfloat16)
    turns = (filled * BLOCK + 2 * CHUNK - 1) // (2 * CHUNK)
    gain[:, columns_at(turns * 2 * CHUNK, WIDE)] = jnp.zeros((BLOCK, WIDE), jnp.bfloat16)

    def one_near(s, carry):
        live = near_live[0]
        for other in range(1, count):
            live = jnp.where(s == other, near_live[other], live)

        def weigh_chunk(start, slot, used):
            weigh(
                near_vec.at[s], near_time[s, 0:1, :], far_pattern[:, columns_at(start, CHUNK)], weights.at[slot], used
            )

        def gain_chunk(start, slot, used):
            depth = used * BLOCK
            part = jnp.dot(cats[s, :, 0:depth], weights[slot, 0:depth, :], preferred_element_type=jnp.float32)
            gain[:, columns_at(start, CHUNK)] = part.astype(jnp.bfloat16)

        for used in range(1, SLOTS + 1):

            @pl.when(live == used)
            def _(used=used):
                def turn(i, carry):
                    start = i * 2 * CHUNK
                    weigh_chunk(start, 0, used)
                    gain_chunk(jnp.maximum(start - CHUNK, 0), 1, used)
                    weigh_chunk(start + CHUNK, 1, used)
                    gain_chunk(start, 0, used)
                    return carry

                lax.fori_loop(0, turns, turn, 0)
                gain_chunk(turns * 2 * CHUNK - CHUNK, 1, used)

        for r in range(n_far):
            tiles[s * n_far + r] = lax.dot_general(
                gain[:, columns_at(starts[r], WIDE)],
                far[r, 0:BLOCK, :],
                (((1,), (1,)), ((), ())),
                preferred_element_type=jnp.float32,
            ).astype(tiles.dtype)
        return carry

    lax.fori_loop(0, count, one_near, 0)
    for u in range(count * n_far):
        s, r = u // n_far, u % n_far
        outs[s][:, r * BLOCK : (r + 1) * BLOCK] = tiles[u]
    if placing:
        last = spread(own, out, 2 * own.shape[1], pair_start(x, odd), sems.at[2])
        for copy in last:
            copy.start()
        for copy in copies + last:
            copy.wait()


def make_tiles(blocks, far, dtype, arrived=()):
    count, n_far = len(blocks), far.shape[0]
    vmem = pl.BlockSpec(memory_space=pltpu.VMEM)
    width = n_far * BLOCK
    scratch = [
        pltpu.VMEM((DEPTH, WIDE), jnp.float32),
        pltpu.VMEM((count, WIDE, DEPTH), jnp.bfloat16),
        pltpu.VMEM((count, 8, WIDE), jnp.float32),
        pltpu.VMEM((count, BLOCK, WIDE), jnp.bfloat16),
        pltpu.VMEM((PATTERN, (n_far + 2) * WIDE), jnp.bfloat16),
        pltpu.VMEM((BLOCK, (n_far + 2) * WIDE), jnp.bfloat16),
        pltpu.VMEM((count * n_far, BLOCK, BLOCK), dtype),
        pltpu.VMEM((2, WIDE, CHUNK), jnp.bfloat16),
    ]
    if arrived:
        out_shape = (jax.ShapeDtypeStruct((BLOCK, 4 * width), jnp.float32),)
        scratch += [pltpu.VMEM((BLOCK, width), jnp.float32)] * 3 + [pltpu.SemaphoreType.DMA((3, SIDE * PAIR))]
        out_specs = (pl.BlockSpec(memory_space=pltpu.HBM),)
    else:
        out_shape = (jax.ShapeDtypeStruct((BLOCK, width), dtype),) * count
        out_specs = (vmem,) * count
    return pl.pallas_call(
        functools.partial(tiles_kernel, count, bool(arrived)),
        out_shape=out_shape,
        in_specs=[vmem] * (count + 1 + len(arrived)),
        out_specs=out_specs,
        scratch_shapes=scratch,
        compiler_params=pltpu.CompilerParams(vmem_limit_bytes=16 * 2**20),
        cost_estimate=pl.CostEstimate(
            flops=count * 10**9, bytes_accessed=count * 2 * 10**6, transcendentals=count * 2**22
        ),
        name="make_tiles",
    )(*blocks, far, *arrived)


def pair_start(x, odd):
    return jnp.where(odd, lax.rem((x + 3) // PAIR * PAIR + 1, SIDE), x // PAIR * PAIR)


def spread(source, out, base, start, sems):
    copies = []
    for y in range(SIDE):
        for i in range(PAIR):
            column = base + (y * SIDE + lax.rem(start + i, SIDE)) * BLOCK
            u = y * PAIR + i
            copies.append(
                pltpu.make_async_copy(
                    source.at[:, u * BLOCK : (u + 1) * BLOCK], out.at[:, columns_at(column, BLOCK)], sems.at[u]
                )
            )
    return copies


def where_placed():
    x = lax.rem(lax.axis_index("obs"), SIDE)
    odd = lax.rem(lax.axis_index("tm"), 2) == 1
    return x, odd, pair_start(x, jnp.logical_not(odd))


def place_rest_kernel(partner, filled, out, wide, sems):
    del filled
    x, odd, _ = where_placed()
    wide[...] = partner[...].astype(jnp.float32)
    copies = spread(wide, out, 2 * wide.shape[1], pair_start(x, odd) + PAIR, sems)
    for copy in copies:
        copy.start()
    for copy in copies:
        copy.wait()


def place_rest(partner, filled):
    hbm = pl.BlockSpec(memory_space=pltpu.HBM)
    return pl.pallas_call(
        place_rest_kernel,
        out_shape=jax.ShapeDtypeStruct(filled.shape, filled.dtype),
        in_specs=[pl.BlockSpec(memory_space=pltpu.VMEM), hbm],
        out_specs=hbm,
        input_output_aliases={1: 0},
        scratch_shapes=[pltpu.VMEM(partner.shape, jnp.float32), pltpu.SemaphoreType.DMA((SIDE * PAIR,))],
        compiler_params=pltpu.CompilerParams(vmem_limit_bytes=12 * 2**20),
        name="place_rest",
    )(partner, filled)


def on_device(footprints, block_times, block_cells, live_counts, cell_lat, cell_lon):
    group = lax.axis_size("obs")
    spans = lax.axis_size("tm")
    axes = ("tm", "obs")
    sides = ((0, 1), (2, 3)), ((1, 2), (3, 0))
    near_by = [
        [t * group + y * SIDE + x for y in range(group // SIDE) for x in pair]
        for t in range(spans)
        for pair in sides[t % 2]
    ]

    def across(t, o):
        x = o % SIDE
        return o - x + (x ^ 1 if t % 2 else SIDE - 1 - x)

    def steps(by, crossing):
        pairs = []
        for t in range(spans):
            if 0 <= t + by < spans:
                for o in range(group):
                    other = across(min(t, t + by), o) if crossing else o
                    pairs.append((t * group + o, (t + by) * group + other))
        return pairs

    lat = cell_lat.reshape(-1, BLOCK)
    lon = cell_lon.reshape(-1, BLOCK)
    block, payload = make_block(
        footprints, block_times, block_cells, live_counts, lat, lon, group // (SIDE // PAIR)
    )
    far = lax.all_to_all(payload, axes, 0, 0, tiled=True, axis_index_groups=near_by)
    partner_block = lax.ppermute(block, axes, steps(0, True))
    next_block = lax.ppermute(block, axes, steps(-1, False))
    next_partner_block = lax.ppermute(block, axes, steps(-1, True))
    footprint_cov = self_gain(block)
    far, footprint_cov = lax.optimization_barrier((far, footprint_cov))
    (next_partner_tiles,) = make_tiles((next_partner_block,), far, jnp.bfloat16)
    before_partner = lax.ppermute(next_partner_tiles, axes, steps(1, True))
    (partner_tiles,) = make_tiles((partner_block,), far, jnp.bfloat16)
    partner = lax.ppermute(partner_tiles, axes, steps(0, True))
    (next_tiles,) = make_tiles((next_block,), far, jnp.bfloat16)
    before = lax.ppermute(next_tiles, axes, steps(1, False))
    (filled,) = make_tiles((block,), far, jnp.float32, (before, before_partner))
    cross_cov = place_rest(partner, filled)
    return (cross_cov, footprint_cov)


def solution(mesh):
    placed = (
        P(("tm", "obs"), None, None, None),
        P(("tm", "obs"), None),
        P(("tm", "obs"), None),
        P(("tm", "obs")),
        P(),
        P(),
    )
    return jax.shard_map(
        on_device,
        mesh=mesh,
        in_specs=placed,
        out_specs=(P(("tm", "obs"), None), P(("tm", "obs"), None, None, None)),
        check_vma=False,
    )
```

```python
import functools
import math

import jax
import jax.numpy as jnp
from jax import lax
from jax.experimental import pallas as pl
from jax.experimental.pallas import tpu as pltpu
from jax.sharding import PartitionSpec as P

BLOCK = 128
SLOTS = 4
WIDE = SLOTS * BLOCK
PATTERN = 16
ROWS = BLOCK + PATTERN
PARTS = 3
DEPTH = PARTS * PATTERN
ONE_ROW = 9
TIME_ROW = 10
LIVE_ROW = 11
CHUNK = WIDE
TSTEP = 8
CORR = 0.6
SCALE = (math.log2(math.e) / CORR) ** 2
DECAY = math.log2(math.e) / TSTEP
TINY = 1e-12
RADIANS = math.pi / 180.0
SIDE = 4
PAIR = 2


def rounded(x):
    return x.astype(jnp.bfloat16).astype(jnp.float32)


def split3(x):
    high = rounded(x)
    mid = rounded(x - high)
    return high, mid, rounded(x - high - mid)


def block_kernel(
    prints, times, cells, live, lat_ref, lon_ref, block, payload, own, when, where, alive, lat, lon, cat, rows, pattern, loads_sem, sends_sem
):
    loads = [
        pltpu.make_async_copy(source, target, loads_sem.at[i])
        for i, (source, target) in enumerate(
            ((prints, own), (live, alive), (cells, where), (times, when), (lat_ref, lat), (lon_ref, lon))
        )
    ]
    for load in loads:
        load.start()
    targets = [payload.at[i] for i in range(payload.shape[0])] + [block.at[0]]

    def send(source, start, size, sem):
        copies = [
            pltpu.make_async_copy(source, target.at[pl.ds(start, size), :], sends_sem.at[sem, i])
            for i, target in enumerate(targets)
        ]
        for copy in copies:
            copy.start()
        return copies

    base = lax.axis_index("tm") * TSTEP
    loads[0].wait()
    loads[1].wait()
    for j in range(SLOTS):
        kept = jnp.where(j < alive[0], own[0, j], jnp.zeros((BLOCK, BLOCK), jnp.bfloat16))
        cat[0:BLOCK, j * BLOCK : (j + 1) * BLOCK] = kept
    sends = send(cat.at[pl.ds(0, BLOCK), :], 0, BLOCK, 0)
    for load in loads[2:]:
        load.wait()
    pattern[...] = jnp.zeros_like(pattern)
    pattern[pl.ds(ONE_ROW, 1), :] = jnp.ones((1, WIDE), jnp.float32)
    pattern[pl.ds(LIVE_ROW, 1), :] = jnp.full((1, WIDE), alive[0].astype(jnp.float32))
    for j in range(SLOTS):
        moment = (base + when[0, j]).astype(jnp.float32)
        pattern[pl.ds(TIME_ROW, 1), j * BLOCK : (j + 1) * BLOCK] = jnp.full((1, BLOCK), moment)
        rows[pl.ds(j, 1), :] = lat[pl.ds(where[0, j], 1), :]
        rows[pl.ds(SLOTS + j, 1), :] = lon[pl.ds(where[0, j], 1), :]
    degrees = rows[...].astype(jnp.float32)
    is_lat = lax.broadcasted_iota(jnp.int32, degrees.shape, 0) < SLOTS
    angles = (degrees + jnp.where(is_lat, -89.5, 0.5)) * RADIANS
    cosines, sines = jnp.cos(angles), jnp.sin(angles)
    across = cosines[0:SLOTS]
    units = (across * cosines[SLOTS:], across * sines[SLOTS:], sines[0:SLOTS])
    for c, unit in enumerate(units):
        for part, value in enumerate(split3(unit)):
            for j in range(SLOTS):
                pattern[pl.ds(PARTS * c + part, 1), j * BLOCK : (j + 1) * BLOCK] = value[j : j + 1]
    cat[BLOCK:ROWS, :] = pattern[...].astype(jnp.bfloat16)
    sends += send(cat.at[pl.ds(BLOCK, PATTERN), :], BLOCK, PATTERN, 1)
    for copy in sends:
        copy.wait()


def make_block(footprints, times, cells, live, lat, lon, count):
    hbm = pl.BlockSpec(memory_space=pltpu.HBM)
    return pl.pallas_call(
        block_kernel,
        out_shape=(
            jax.ShapeDtypeStruct((1, ROWS, WIDE), jnp.bfloat16),
            jax.ShapeDtypeStruct((count, ROWS, WIDE), jnp.bfloat16),
        ),
        in_specs=[hbm] * 6,
        out_specs=(hbm, hbm),
        scratch_shapes=[
            pltpu.VMEM((1, SLOTS, BLOCK, BLOCK), jnp.bfloat16),
            pltpu.SMEM((1, SLOTS), jnp.int32),
            pltpu.SMEM((1, SLOTS), jnp.int32),
            pltpu.SMEM((1,), jnp.int32),
            pltpu.VMEM(lat.shape, jnp.int32),
            pltpu.VMEM(lon.shape, jnp.int32),
            pltpu.VMEM((ROWS, WIDE), jnp.bfloat16),
            pltpu.VMEM((2 * SLOTS, BLOCK), jnp.int32),
            pltpu.VMEM((PATTERN, WIDE), jnp.float32),
            pltpu.SemaphoreType.DMA((6,)),
            pltpu.SemaphoreType.DMA((2, count + 1)),
        ],
        compiler_params=pltpu.CompilerParams(vmem_limit_bytes=60 * 2**20),
        name="make_block",
    )(footprints, times, cells, live, lat, lon)


def prepare_near(block, near_rows):
    pattern = block[0, BLOCK:ROWS, :].astype(jnp.float32)
    near_rows[...] = jnp.zeros_like(near_rows)
    for c in range(3):
        high, mid, low = (pattern[PARTS * c + part : PARTS * c + part + 1] for part in range(PARTS))
        scaled = split3((high + mid + low) * (-2.0 * SCALE))
        for segment, value in enumerate(scaled):
            for part in range(PARTS - segment):
                near_rows[pl.ds(segment * PATTERN + PARTS * c + part, 1), :] = value
    ends = split3(jnp.full((1, WIDE), 2.0 * SCALE, jnp.float32))
    for segment, value in enumerate(ends):
        near_rows[pl.ds(segment * PATTERN + ONE_ROW, 1), :] = value
    near_rows[pl.ds(TIME_ROW, 1), :] = jnp.zeros((1, WIDE), jnp.float32)
    return near_rows[...].T.astype(jnp.bfloat16), pattern[TIME_ROW : TIME_ROW + 1]


def weigh(near_vec, near_time, far_pattern, weights, live):
    columns = far_pattern.shape[1]
    far_vec = jnp.concatenate([far_pattern] * PARTS, axis=0)
    far_time = far_pattern.astype(jnp.float32)[TIME_ROW : TIME_ROW + 1]
    for k in range(live):
        rows = pl.ds(k * BLOCK, BLOCK)
        own = jnp.concatenate([near_time[:, k * BLOCK : (k + 1) * BLOCK]] * (columns // BLOCK), axis=1)
        lag = jnp.abs(own - far_time) * (-DECAY)
        square = jnp.maximum(jnp.dot(near_vec[rows, :], far_vec, preferred_element_type=jnp.float32), TINY)
        weights[rows, :] = jnp.exp2(lag - square * lax.rsqrt(square)).astype(jnp.bfloat16)


def local_kernel(*refs):
    *blocks, cov, local, near_rows, near_vec, weights = refs
    last = len(blocks) - 1
    own = blocks[last]
    far_pattern = own[0, BLOCK:ROWS, :]

    def weigh_near(s):
        near_vec[s], when = prepare_near(blocks[s], near_rows)
        weigh(near_vec.at[s], when, far_pattern, weights.at[s % 2], SLOTS)

    def finish(s):
        gain = jnp.dot(blocks[s][0, 0:BLOCK, :], weights[s % 2], preferred_element_type=jnp.float32)
        if s == last:
            for j in range(SLOTS):
                cov[0, j] = gain[:, j * BLOCK : (j + 1) * BLOCK]
        local[s] = lax.dot_general(
            gain.astype(jnp.bfloat16),
            own[0, 0:BLOCK, :],
            (((1,), (1,)), ((), ())),
            preferred_element_type=jnp.float32,
        )

    for s in range(last + 1):
        weigh_near(s)
        if s:
            finish(s - 1)
    finish(last)


def make_local(*blocks):
    vmem = pl.BlockSpec(memory_space=pltpu.VMEM)
    return pl.pallas_call(
        local_kernel,
        out_shape=(
            jax.ShapeDtypeStruct((1, SLOTS, BLOCK, BLOCK), jnp.float32),
            jax.ShapeDtypeStruct((len(blocks), BLOCK, BLOCK), jnp.float32),
        ),
        in_specs=[vmem] * len(blocks),
        out_specs=(vmem, vmem),
        scratch_shapes=[
            pltpu.VMEM((DEPTH, WIDE), jnp.float32),
            pltpu.VMEM((len(blocks), WIDE, DEPTH), jnp.bfloat16),
            pltpu.VMEM((2, WIDE, WIDE), jnp.bfloat16),
        ],
        compiler_params=pltpu.CompilerParams(vmem_limit_bytes=12 * 2**20),
        cost_estimate=pl.CostEstimate(flops=4 * 10**9, bytes_accessed=10**6, transcendentals=2**21),
        name="make_local",
    )(*blocks)


def live_of(pattern):
    count = pattern[:, 0:BLOCK].astype(jnp.float32)[LIVE_ROW : LIVE_ROW + 1]
    return jnp.max(count).astype(jnp.int32)


def columns_at(start, width):
    return pl.ds(pl.multiple_of(start, BLOCK), width)


def tiles_kernel(count, base, placing, *refs):
    blocks, (far, local), refs = refs[:count], refs[count : count + 2], refs[count + 2 :]
    x, odd, earlier = where_placed()
    row = lax.axis_index("obs") // SIDE
    mine = row * PAIR + lax.rem(x - pair_start(x, odd) + SIDE, SIDE)
    known = base >= 0
    if placing:
        before, before_partner, out, *scratch, wide, wide_partner, own, sems = refs
        outs = (own,)
        wide[...] = before[...].astype(jnp.float32)
        wide_partner[...] = before_partner[...].astype(jnp.float32)
        copies = spread(wide, out, 0, earlier, sems.at[0])
        copies += spread(wide_partner, out, 0, earlier + PAIR, sems.at[1])
        for copy in copies:
            copy.start()
    else:
        outs, scratch = refs[:count], refs[count:]
    near_rows, near_vec, near_time, cats, far_pattern, gain, tiles, weights = scratch
    n_far = far.shape[0]
    near_live = []
    for s in range(count):
        vec, when = prepare_near(blocks[s], near_rows)
        near_vec[s] = vec
        near_time[s] = jnp.broadcast_to(when, near_time.shape[1:])
        cats[s] = blocks[s][0, 0:BLOCK, :]
        near_live.append(live_of(blocks[s][0, BLOCK:ROWS, :]))
    starts, filled = [], jnp.int32(0)
    for r in range(n_far):
        pattern = far[r, BLOCK:ROWS, :]
        far_pattern[:, columns_at(filled * BLOCK, WIDE)] = pattern
        starts.append(filled * BLOCK)
        filled = filled + (jnp.where(r == mine, 0, live_of(pattern)) if known else live_of(pattern))
    far_pattern[:, columns_at(filled * BLOCK, WIDE)] = jnp.zeros((PATTERN, WIDE), jnp.bfloat16)
    chunks = (filled * BLOCK + CHUNK - 1) // CHUNK
    turns = chunks // 2
    gain[:, columns_at(chunks * CHUNK, WIDE)] = jnp.zeros((BLOCK, WIDE), jnp.bfloat16)

    def one_near(s, carry):
        live = near_live[0]
        for other in range(1, count):
            live = jnp.where(s == other, near_live[other], live)

        def weigh_chunk(start, slot, used):
            weigh(
                near_vec.at[s], near_time[s, 0:1, :], far_pattern[:, columns_at(start, CHUNK)], weights.at[slot], used
            )

        def gain_chunk(start, slot, used):
            depth = used * BLOCK
            part = jnp.dot(cats[s, :, 0:depth], weights[slot, 0:depth, :], preferred_element_type=jnp.float32)
            gain[:, columns_at(start, CHUNK)] = part.astype(jnp.bfloat16)

        for used in range(1, SLOTS + 1):

            @pl.when(live == used)
            def _(used=used):
                def turn(i, carry):
                    start = i * 2 * CHUNK
                    weigh_chunk(start, 0, used)
                    gain_chunk(jnp.maximum(start - CHUNK, 0), 1, used)
                    weigh_chunk(start + CHUNK, 1, used)
                    gain_chunk(start, 0, used)
                    return carry

                lax.fori_loop(0, turns, turn, 0)
                rest = turns * 2 * CHUNK

                @pl.when(chunks == 2 * turns)
                def _():
                    gain_chunk(rest - CHUNK, 1, used)

                @pl.when(chunks != 2 * turns)
                def _():
                    weigh_chunk(rest, 0, used)
                    gain_chunk(jnp.maximum(rest - CHUNK, 0), 1, used)
                    gain_chunk(rest, 0, used)

        for r in range(n_far):
            tile = lax.dot_general(
                gain[:, columns_at(starts[r], WIDE)],
                far[r, 0:BLOCK, :],
                (((1,), (1,)), ((), ())),
                preferred_element_type=jnp.float32,
            )
            if known:
                tile = jnp.where(r == mine, local[base + s], tile)
            if count == 1:
                outs[0][:, r * BLOCK : (r + 1) * BLOCK] = tile.astype(outs[0].dtype)
                if placing:
                    last[r].start()
            else:
                tiles[s * n_far + r] = tile.astype(tiles.dtype)
        return carry

    if placing:
        last = spread(own, out, 2 * own.shape[1], pair_start(x, odd), sems.at[2])
    if count == 1:
        one_near(0, 0)
    else:
        lax.fori_loop(0, count, one_near, 0)
        for u in range(count * n_far):
            s, r = u // n_far, u % n_far
            outs[s][:, r * BLOCK : (r + 1) * BLOCK] = tiles[u]
    if placing:
        for copy in copies + last:
            copy.wait()


def make_tiles(blocks, base, far, local, dtype, arrived=()):
    count, n_far = len(blocks), far.shape[0]
    vmem = pl.BlockSpec(memory_space=pltpu.VMEM)
    width = n_far * BLOCK
    scratch = [
        pltpu.VMEM((DEPTH, WIDE), jnp.float32),
        pltpu.VMEM((count, WIDE, DEPTH), jnp.bfloat16),
        pltpu.VMEM((count, 8, WIDE), jnp.float32),
        pltpu.VMEM((count, BLOCK, WIDE), jnp.bfloat16),
        pltpu.VMEM((PATTERN, (n_far + 2) * WIDE), jnp.bfloat16),
        pltpu.VMEM((BLOCK, (n_far + 2) * WIDE), jnp.bfloat16),
        pltpu.VMEM((count * n_far, BLOCK, BLOCK), dtype),
        pltpu.VMEM((2, WIDE, CHUNK), jnp.bfloat16),
    ]
    if arrived:
        out_shape = (jax.ShapeDtypeStruct((BLOCK, 4 * width), jnp.float32),)
        scratch += [pltpu.VMEM((BLOCK, width), jnp.float32)] * 3 + [pltpu.SemaphoreType.DMA((3, SIDE * PAIR))]
        out_specs = (pl.BlockSpec(memory_space=pltpu.HBM),)
    else:
        out_shape = (jax.ShapeDtypeStruct((BLOCK, width), dtype),) * count
        out_specs = (vmem,) * count
    return pl.pallas_call(
        functools.partial(tiles_kernel, count, base, bool(arrived)),
        out_shape=out_shape,
        in_specs=[vmem] * (count + 2 + len(arrived)),
        out_specs=out_specs,
        scratch_shapes=scratch,
        compiler_params=pltpu.CompilerParams(vmem_limit_bytes=16 * 2**20),
        cost_estimate=pl.CostEstimate(
            flops=count * 10**9, bytes_accessed=count * 2 * 10**6, transcendentals=count * 2**22
        ),
        name="make_tiles",
    )(*blocks, far, local, *arrived)


def pair_start(x, odd):
    return jnp.where(odd, lax.rem((x + 3) // PAIR * PAIR + 1, SIDE), x // PAIR * PAIR)


def spread(source, out, base, start, sems):
    copies = []
    for y in range(SIDE):
        for i in range(PAIR):
            column = base + (y * SIDE + lax.rem(start + i, SIDE)) * BLOCK
            u = y * PAIR + i
            copies.append(
                pltpu.make_async_copy(
                    source.at[:, u * BLOCK : (u + 1) * BLOCK], out.at[:, columns_at(column, BLOCK)], sems.at[u]
                )
            )
    return copies


def where_placed():
    x = lax.rem(lax.axis_index("obs"), SIDE)
    odd = lax.rem(lax.axis_index("tm"), 2) == 1
    return x, odd, pair_start(x, jnp.logical_not(odd))


def place_rest_kernel(partner, filled, out, wide, sems):
    del filled
    x, odd, _ = where_placed()
    wide[...] = partner[...].astype(jnp.float32)
    copies = spread(wide, out, 2 * wide.shape[1], pair_start(x, odd) + PAIR, sems)
    for copy in copies:
        copy.start()
    for copy in copies:
        copy.wait()


def place_rest(partner, filled):
    hbm = pl.BlockSpec(memory_space=pltpu.HBM)
    return pl.pallas_call(
        place_rest_kernel,
        out_shape=jax.ShapeDtypeStruct(filled.shape, filled.dtype),
        in_specs=[pl.BlockSpec(memory_space=pltpu.VMEM), hbm],
        out_specs=hbm,
        input_output_aliases={1: 0},
        scratch_shapes=[pltpu.VMEM(partner.shape, jnp.float32), pltpu.SemaphoreType.DMA((SIDE * PAIR,))],
        compiler_params=pltpu.CompilerParams(vmem_limit_bytes=12 * 2**20),
        name="place_rest",
    )(partner, filled)


def on_device(footprints, block_times, block_cells, live_counts, cell_lat, cell_lon):
    group = lax.axis_size("obs")
    spans = lax.axis_size("tm")
    axes = ("tm", "obs")
    sides = ((0, 1), (2, 3)), ((1, 2), (3, 0))
    near_by = [
        [t * group + y * SIDE + x for y in range(group // SIDE) for x in pair]
        for t in range(spans)
        for pair in sides[t % 2]
    ]

    def across(t, o):
        x = o % SIDE
        return o - x + (x ^ 1 if t % 2 else SIDE - 1 - x)

    def steps(by, crossing):
        pairs = []
        for t in range(spans):
            if 0 <= t + by < spans:
                for o in range(group):
                    other = across(min(t, t + by), o) if crossing else o
                    pairs.append((t * group + o, (t + by) * group + other))
        return pairs

    lat = cell_lat.reshape(-1, BLOCK)
    lon = cell_lon.reshape(-1, BLOCK)
    block, payload = make_block(
        footprints, block_times, block_cells, live_counts, lat, lon, group // (SIDE // PAIR)
    )
    far = lax.all_to_all(payload, axes, 0, 0, tiled=True, axis_index_groups=near_by)
    partner_block = lax.ppermute(block, axes, steps(0, True))
    next_block = lax.ppermute(block, axes, steps(-1, False))
    next_partner_block = lax.ppermute(block, axes, steps(-1, True))
    footprint_cov, local = make_local(partner_block, block)
    far, local = lax.optimization_barrier((far, local))
    (next_partner_tiles,) = make_tiles((next_partner_block,), -1, far, local, jnp.bfloat16)
    (next_tiles,) = make_tiles((next_block,), -1, far, local, jnp.bfloat16)
    before_partner = lax.ppermute(next_partner_tiles, axes, steps(1, True))
    before = lax.ppermute(next_tiles, axes, steps(1, False))
    (partner_tiles,) = make_tiles((partner_block,), 0, far, local, jnp.bfloat16)
    partner = lax.ppermute(partner_tiles, axes, steps(0, True))
    (filled,) = make_tiles((block,), 1, far, local, jnp.float32, (before, before_partner))
    cross_cov = place_rest(partner, filled)
    return (cross_cov, footprint_cov)


def solution(mesh):
    placed = (
        P(("tm", "obs"), None, None, None),
        P(("tm", "obs"), None),
        P(("tm", "obs"), None),
        P(("tm", "obs")),
        P(),
        P(),
    )
    return jax.shard_map(
        on_device,
        mesh=mesh,
        in_specs=placed,
        out_specs=(P(("tm", "obs"), None), P(("tm", "obs"), None, None, None)),
        check_vma=False,
    )
```

```python
import functools
import math

import jax
import jax.numpy as jnp
from jax import lax
from jax.experimental import pallas as pl
from jax.experimental.pallas import tpu as pltpu
from jax.sharding import PartitionSpec as P

BLOCK = 128
SLOTS = 4
WIDE = SLOTS * BLOCK
PATTERN = 16
ROWS = BLOCK + PATTERN
PARTS = 3
DEPTH = PARTS * PATTERN
ONE_ROW = 9
TIME_ROW = 10
LIVE_ROW = 11
CHUNK = WIDE
TSTEP = 8
CORR = 0.6
SCALE = (math.log2(math.e) / CORR) ** 2
DECAY = math.log2(math.e) / TSTEP
TINY = 1e-12
RADIANS = math.pi / 180.0
SIDE = 4
PAIR = 2


def rounded(x):
    return x.astype(jnp.bfloat16).astype(jnp.float32)


def split3(x):
    high = rounded(x)
    mid = rounded(x - high)
    return high, mid, rounded(x - high - mid)


def block_kernel(
    prints, times, cells, live, lat_ref, lon_ref, block, payload, own, when, where, alive, lat, lon, cat, rows, pattern, loads_sem, sends_sem
):
    loads = [
        pltpu.make_async_copy(source, target, loads_sem.at[i])
        for i, (source, target) in enumerate(
            ((prints, own), (live, alive), (cells, where), (times, when), (lat_ref, lat), (lon_ref, lon))
        )
    ]
    for load in loads:
        load.start()
    targets = [payload.at[i] for i in range(payload.shape[0])] + [block.at[0]]

    def send(source, start, size, sem):
        copies = [
            pltpu.make_async_copy(source, target.at[pl.ds(start, size), :], sends_sem.at[sem, i])
            for i, target in enumerate(targets)
        ]
        for copy in copies:
            copy.start()
        return copies

    base = lax.axis_index("tm") * TSTEP
    loads[0].wait()
    loads[1].wait()
    for j in range(SLOTS):
        kept = jnp.where(j < alive[0], own[0, j], jnp.zeros((BLOCK, BLOCK), jnp.bfloat16))
        cat[0:BLOCK, j * BLOCK : (j + 1) * BLOCK] = kept
    sends = send(cat.at[pl.ds(0, BLOCK), :], 0, BLOCK, 0)
    for load in loads[2:]:
        load.wait()
    pattern[...] = jnp.zeros_like(pattern)
    pattern[pl.ds(ONE_ROW, 1), :] = jnp.ones((1, WIDE), jnp.float32)
    pattern[pl.ds(LIVE_ROW, 1), :] = jnp.full((1, WIDE), alive[0].astype(jnp.float32))
    for j in range(SLOTS):
        moment = (base + when[0, j]).astype(jnp.float32)
        pattern[pl.ds(TIME_ROW, 1), j * BLOCK : (j + 1) * BLOCK] = jnp.full((1, BLOCK), moment)
        rows[pl.ds(j, 1), :] = lat[pl.ds(where[0, j], 1), :]
        rows[pl.ds(SLOTS + j, 1), :] = lon[pl.ds(where[0, j], 1), :]
    degrees = rows[...].astype(jnp.float32)
    is_lat = lax.broadcasted_iota(jnp.int32, degrees.shape, 0) < SLOTS
    angles = (degrees + jnp.where(is_lat, -89.5, 0.5)) * RADIANS
    cosines, sines = jnp.cos(angles), jnp.sin(angles)
    across = cosines[0:SLOTS]
    units = (across * cosines[SLOTS:], across * sines[SLOTS:], sines[0:SLOTS])
    for c, unit in enumerate(units):
        for part, value in enumerate(split3(unit)):
            for j in range(SLOTS):
                pattern[pl.ds(PARTS * c + part, 1), j * BLOCK : (j + 1) * BLOCK] = value[j : j + 1]
    cat[BLOCK:ROWS, :] = pattern[...].astype(jnp.bfloat16)
    sends += send(cat.at[pl.ds(BLOCK, PATTERN), :], BLOCK, PATTERN, 1)
    for copy in sends:
        copy.wait()


def make_block(footprints, times, cells, live, lat, lon, count):
    hbm = pl.BlockSpec(memory_space=pltpu.HBM)
    return pl.pallas_call(
        block_kernel,
        out_shape=(
            jax.ShapeDtypeStruct((1, ROWS, WIDE), jnp.bfloat16),
            jax.ShapeDtypeStruct((count, ROWS, WIDE), jnp.bfloat16),
        ),
        in_specs=[hbm] * 6,
        out_specs=(hbm, hbm),
        scratch_shapes=[
            pltpu.VMEM((1, SLOTS, BLOCK, BLOCK), jnp.bfloat16),
            pltpu.SMEM((1, SLOTS), jnp.int32),
            pltpu.SMEM((1, SLOTS), jnp.int32),
            pltpu.SMEM((1,), jnp.int32),
            pltpu.VMEM(lat.shape, jnp.int32),
            pltpu.VMEM(lon.shape, jnp.int32),
            pltpu.VMEM((ROWS, WIDE), jnp.bfloat16),
            pltpu.VMEM((2 * SLOTS, BLOCK), jnp.int32),
            pltpu.VMEM((PATTERN, WIDE), jnp.float32),
            pltpu.SemaphoreType.DMA((6,)),
            pltpu.SemaphoreType.DMA((2, count + 1)),
        ],
        compiler_params=pltpu.CompilerParams(vmem_limit_bytes=60 * 2**20),
        name="make_block",
    )(footprints, times, cells, live, lat, lon)


def prepare_near(block, near_rows):
    pattern = block[0, BLOCK:ROWS, :].astype(jnp.float32)
    near_rows[...] = jnp.zeros_like(near_rows)
    for c in range(3):
        high, mid, low = (pattern[PARTS * c + part : PARTS * c + part + 1] for part in range(PARTS))
        scaled = split3((high + mid + low) * (-2.0 * SCALE))
        for segment, value in enumerate(scaled):
            for part in range(PARTS - segment):
                near_rows[pl.ds(segment * PATTERN + PARTS * c + part, 1), :] = value
    ends = split3(jnp.full((1, WIDE), 2.0 * SCALE, jnp.float32))
    for segment, value in enumerate(ends):
        near_rows[pl.ds(segment * PATTERN + ONE_ROW, 1), :] = value
    near_rows[pl.ds(TIME_ROW, 1), :] = jnp.zeros((1, WIDE), jnp.float32)
    return near_rows[...].T.astype(jnp.bfloat16), pattern[TIME_ROW : TIME_ROW + 1]


def weigh(near_vec, near_time, far_pattern, weights, live):
    columns = far_pattern.shape[1]
    far_vec = jnp.concatenate([far_pattern] * PARTS, axis=0)
    far_time = far_pattern.astype(jnp.float32)[TIME_ROW : TIME_ROW + 1]
    for k in range(live):
        rows = pl.ds(k * BLOCK, BLOCK)
        own = jnp.concatenate([near_time[:, k * BLOCK : (k + 1) * BLOCK]] * (columns // BLOCK), axis=1)
        lag = jnp.abs(own - far_time) * (-DECAY)
        square = jnp.maximum(jnp.dot(near_vec[rows, :], far_vec, preferred_element_type=jnp.float32), TINY)
        weights[rows, :] = jnp.exp2(lag - square * lax.rsqrt(square)).astype(jnp.bfloat16)


def local_kernel(*refs):
    *blocks, cov, local, near_rows, near_vec, weights = refs
    last = len(blocks) - 1
    own = blocks[last]
    far_pattern = own[0, BLOCK:ROWS, :]

    def weigh_near(s):
        near_vec[s], when = prepare_near(blocks[s], near_rows)
        weigh(near_vec.at[s], when, far_pattern, weights.at[s % 2], SLOTS)

    def finish(s):
        gain = jnp.dot(blocks[s][0, 0:BLOCK, :], weights[s % 2], preferred_element_type=jnp.float32)
        if s == last:
            for j in range(SLOTS):
                cov[0, j] = gain[:, j * BLOCK : (j + 1) * BLOCK]
        local[s] = lax.dot_general(
            gain.astype(jnp.bfloat16),
            own[0, 0:BLOCK, :],
            (((1,), (1,)), ((), ())),
            preferred_element_type=jnp.float32,
        )

    for s in range(last + 1):
        weigh_near(s)
        if s:
            finish(s - 1)
    finish(last)


def make_local(*blocks):
    vmem = pl.BlockSpec(memory_space=pltpu.VMEM)
    return pl.pallas_call(
        local_kernel,
        out_shape=(
            jax.ShapeDtypeStruct((1, SLOTS, BLOCK, BLOCK), jnp.float32),
            jax.ShapeDtypeStruct((len(blocks), BLOCK, BLOCK), jnp.float32),
        ),
        in_specs=[vmem] * len(blocks),
        out_specs=(vmem, vmem),
        scratch_shapes=[
            pltpu.VMEM((DEPTH, WIDE), jnp.float32),
            pltpu.VMEM((len(blocks), WIDE, DEPTH), jnp.bfloat16),
            pltpu.VMEM((2, WIDE, WIDE), jnp.bfloat16),
        ],
        compiler_params=pltpu.CompilerParams(vmem_limit_bytes=12 * 2**20),
        cost_estimate=pl.CostEstimate(flops=4 * 10**9, bytes_accessed=10**6, transcendentals=2**21),
        name="make_local",
    )(*blocks)


def live_of(pattern):
    count = pattern[:, 0:BLOCK].astype(jnp.float32)[LIVE_ROW : LIVE_ROW + 1]
    return jnp.max(count).astype(jnp.int32)


def columns_at(start, width):
    return pl.ds(pl.multiple_of(start, BLOCK), width)


def tiles_kernel(count, base, placing, *refs):
    blocks, (far, local), refs = refs[:count], refs[count : count + 2], refs[count + 2 :]
    x, odd, earlier = where_placed()
    row = lax.axis_index("obs") // SIDE
    mine = row * PAIR + lax.rem(x - pair_start(x, odd) + SIDE, SIDE)
    known = base >= 0
    if placing:
        before_partner, partner, out, *scratch, wide, wide_partner, own, sems = refs
        outs = (own,)
        wide[...] = before_partner[...].astype(jnp.float32)
        wide_partner[...] = partner[...].astype(jnp.float32)
        copies = spread(wide, out, 0, earlier + PAIR, sems.at[0])
        copies += spread(wide_partner, out, 2 * own.shape[1], pair_start(x, odd) + PAIR, sems.at[1])
        for copy in copies:
            copy.start()
    else:
        outs, scratch = refs[:count], refs[count:]
    near_rows, near_vec, near_time, cats, far_pattern, gain, tiles, weights = scratch
    n_far = far.shape[0]
    near_live = []
    for s in range(count):
        vec, when = prepare_near(blocks[s], near_rows)
        near_vec[s] = vec
        near_time[s] = jnp.broadcast_to(when, near_time.shape[1:])
        cats[s] = blocks[s][0, 0:BLOCK, :]
        near_live.append(live_of(blocks[s][0, BLOCK:ROWS, :]))
    starts, filled = [], jnp.int32(0)
    for r in range(n_far):
        pattern = far[r, BLOCK:ROWS, :]
        far_pattern[:, columns_at(filled * BLOCK, WIDE)] = pattern
        starts.append(filled * BLOCK)
        filled = filled + (jnp.where(r == mine, 0, live_of(pattern)) if known else live_of(pattern))
    far_pattern[:, columns_at(filled * BLOCK, WIDE)] = jnp.zeros((PATTERN, WIDE), jnp.bfloat16)
    chunks = (filled * BLOCK + CHUNK - 1) // CHUNK
    turns = chunks // 2
    gain[:, columns_at(chunks * CHUNK, WIDE)] = jnp.zeros((BLOCK, WIDE), jnp.bfloat16)

    def one_near(s, carry):
        live = near_live[0]
        for other in range(1, count):
            live = jnp.where(s == other, near_live[other], live)

        def weigh_chunk(start, slot, used):
            weigh(
                near_vec.at[s], near_time[s, 0:1, :], far_pattern[:, columns_at(start, CHUNK)], weights.at[slot], used
            )

        def gain_chunk(start, slot, used):
            depth = used * BLOCK
            part = jnp.dot(cats[s, :, 0:depth], weights[slot, 0:depth, :], preferred_element_type=jnp.float32)
            gain[:, columns_at(start, CHUNK)] = part.astype(jnp.bfloat16)

        for used in range(1, SLOTS + 1):

            @pl.when(live == used)
            def _(used=used):
                def turn(i, carry):
                    start = i * 2 * CHUNK
                    weigh_chunk(start, 0, used)
                    gain_chunk(jnp.maximum(start - CHUNK, 0), 1, used)
                    weigh_chunk(start + CHUNK, 1, used)
                    gain_chunk(start, 0, used)
                    return carry

                lax.fori_loop(0, turns, turn, 0)
                rest = turns * 2 * CHUNK

                @pl.when(chunks == 2 * turns)
                def _():
                    gain_chunk(rest - CHUNK, 1, used)

                @pl.when(chunks != 2 * turns)
                def _():
                    weigh_chunk(rest, 0, used)
                    gain_chunk(jnp.maximum(rest - CHUNK, 0), 1, used)
                    gain_chunk(rest, 0, used)

        for r in range(n_far):
            tile = lax.dot_general(
                gain[:, columns_at(starts[r], WIDE)],
                far[r, 0:BLOCK, :],
                (((1,), (1,)), ((), ())),
                preferred_element_type=jnp.float32,
            )
            if known:
                tile = jnp.where(r == mine, local[base + s], tile)
            if count == 1:
                outs[0][:, r * BLOCK : (r + 1) * BLOCK] = tile.astype(outs[0].dtype)
                if placing:
                    last[r].start()
            else:
                tiles[s * n_far + r] = tile.astype(tiles.dtype)
        return carry

    if placing:
        last = spread(own, out, 2 * own.shape[1], pair_start(x, odd), sems.at[2])
    if count == 1:
        one_near(0, 0)
    else:
        lax.fori_loop(0, count, one_near, 0)
        for u in range(count * n_far):
            s, r = u // n_far, u % n_far
            outs[s][:, r * BLOCK : (r + 1) * BLOCK] = tiles[u]
    if placing:
        for copy in copies + last:
            copy.wait()


def make_tiles(blocks, base, far, local, dtype, arrived=()):
    count, n_far = len(blocks), far.shape[0]
    vmem = pl.BlockSpec(memory_space=pltpu.VMEM)
    width = n_far * BLOCK
    scratch = [
        pltpu.VMEM((DEPTH, WIDE), jnp.float32),
        pltpu.VMEM((count, WIDE, DEPTH), jnp.bfloat16),
        pltpu.VMEM((count, 8, WIDE), jnp.float32),
        pltpu.VMEM((count, BLOCK, WIDE), jnp.bfloat16),
        pltpu.VMEM((PATTERN, (n_far + 2) * WIDE), jnp.bfloat16),
        pltpu.VMEM((BLOCK, (n_far + 2) * WIDE), jnp.bfloat16),
        pltpu.VMEM((count * n_far, BLOCK, BLOCK), dtype),
        pltpu.VMEM((2, WIDE, CHUNK), jnp.bfloat16),
    ]
    if arrived:
        out_shape = (jax.ShapeDtypeStruct((BLOCK, 4 * width), jnp.float32),)
        scratch += [pltpu.VMEM((BLOCK, width), jnp.float32)] * 3 + [pltpu.SemaphoreType.DMA((3, SIDE * PAIR))]
        out_specs = (pl.BlockSpec(memory_space=pltpu.HBM),)
    else:
        out_shape = (jax.ShapeDtypeStruct((BLOCK, width), dtype),) * count
        out_specs = (vmem,) * count
    return pl.pallas_call(
        functools.partial(tiles_kernel, count, base, bool(arrived)),
        out_shape=out_shape,
        in_specs=[vmem] * (count + 2 + len(arrived)),
        out_specs=out_specs,
        scratch_shapes=scratch,
        compiler_params=pltpu.CompilerParams(vmem_limit_bytes=16 * 2**20),
        cost_estimate=pl.CostEstimate(
            flops=count * 10**9, bytes_accessed=count * 2 * 10**6, transcendentals=count * 2**22
        ),
        name="make_tiles",
    )(*blocks, far, local, *arrived)


def pair_start(x, odd):
    return jnp.where(odd, lax.rem((x + 3) // PAIR * PAIR + 1, SIDE), x // PAIR * PAIR)


def spread(source, out, base, start, sems):
    copies = []
    for y in range(SIDE):
        for i in range(PAIR):
            column = base + (y * SIDE + lax.rem(start + i, SIDE)) * BLOCK
            u = y * PAIR + i
            copies.append(
                pltpu.make_async_copy(
                    source.at[:, u * BLOCK : (u + 1) * BLOCK], out.at[:, columns_at(column, BLOCK)], sems.at[u]
                )
            )
    return copies


def where_placed():
    x = lax.rem(lax.axis_index("obs"), SIDE)
    odd = lax.rem(lax.axis_index("tm"), 2) == 1
    return x, odd, pair_start(x, jnp.logical_not(odd))


def place_rest_kernel(before, filled, out, wide, sems):
    del filled
    wide[...] = before[...].astype(jnp.float32)
    copies = spread(wide, out, 0, where_placed()[2], sems)
    for copy in copies:
        copy.start()
    for copy in copies:
        copy.wait()


def place_rest(before, filled):
    hbm = pl.BlockSpec(memory_space=pltpu.HBM)
    return pl.pallas_call(
        place_rest_kernel,
        out_shape=jax.ShapeDtypeStruct(filled.shape, filled.dtype),
        in_specs=[pl.BlockSpec(memory_space=pltpu.VMEM), hbm],
        out_specs=hbm,
        input_output_aliases={1: 0},
        scratch_shapes=[pltpu.VMEM(before.shape, jnp.float32), pltpu.SemaphoreType.DMA((SIDE * PAIR,))],
        compiler_params=pltpu.CompilerParams(vmem_limit_bytes=12 * 2**20),
        name="place_rest",
    )(before, filled)


def on_device(footprints, block_times, block_cells, live_counts, cell_lat, cell_lon):
    group = lax.axis_size("obs")
    spans = lax.axis_size("tm")
    axes = ("tm", "obs")
    sides = ((0, 1), (2, 3)), ((1, 2), (3, 0))
    near_by = [
        [t * group + y * SIDE + x for y in range(group // SIDE) for x in pair]
        for t in range(spans)
        for pair in sides[t % 2]
    ]

    def across(t, o):
        x = o % SIDE
        return o - x + (x ^ 1 if t % 2 else SIDE - 1 - x)

    def steps(by, crossing):
        pairs = []
        for t in range(spans):
            if 0 <= t + by < spans:
                for o in range(group):
                    other = across(min(t, t + by), o) if crossing else o
                    pairs.append((t * group + o, (t + by) * group + other))
        return pairs

    lat = cell_lat.reshape(-1, BLOCK)
    lon = cell_lon.reshape(-1, BLOCK)
    block, payload = make_block(
        footprints, block_times, block_cells, live_counts, lat, lon, group // (SIDE // PAIR)
    )
    far = lax.all_to_all(payload, axes, 0, 0, tiled=True, axis_index_groups=near_by)
    partner_block = lax.ppermute(block, axes, steps(0, True))
    next_block = lax.ppermute(block, axes, steps(-1, False))
    next_partner_block = lax.ppermute(block, axes, steps(-1, True))
    footprint_cov, local = make_local(partner_block, block)
    far, local = lax.optimization_barrier((far, local))
    (next_partner_tiles,) = make_tiles((next_partner_block,), -1, far, local, jnp.bfloat16)
    before_partner = lax.ppermute(next_partner_tiles, axes, steps(1, True))
    (partner_tiles,) = make_tiles((partner_block,), 0, far, local, jnp.bfloat16)
    partner = lax.ppermute(partner_tiles, axes, steps(0, True))
    far, partner_tiles = lax.optimization_barrier((far, partner_tiles))
    (next_tiles,) = make_tiles((next_block,), -1, far, local, jnp.bfloat16)
    before = lax.ppermute(next_tiles, axes, steps(1, False))
    (filled,) = make_tiles((block,), 1, far, local, jnp.float32, (before_partner, partner))
    cross_cov = place_rest(before, filled)
    return (cross_cov, footprint_cov)


def solution(mesh):
    placed = (
        P(("tm", "obs"), None, None, None),
        P(("tm", "obs"), None),
        P(("tm", "obs"), None),
        P(("tm", "obs")),
        P(),
        P(),
    )
    return jax.shard_map(
        on_device,
        mesh=mesh,
        in_specs=placed,
        out_specs=(P(("tm", "obs"), None), P(("tm", "obs"), None, None, None)),
        check_vma=False,
    )
```

```python
import functools
import math

import jax
import jax.numpy as jnp
from jax import lax
from jax.experimental import pallas as pl
from jax.experimental.pallas import tpu as pltpu
from jax.sharding import PartitionSpec as P

BLOCK = 128
SLOTS = 4
WIDE = SLOTS * BLOCK
PATTERN = 16
ROWS = BLOCK + PATTERN
PARTS = 3
DEPTH = PARTS * PATTERN
ONE_ROW = 9
TIME_ROW = 10
LIVE_ROW = 11
CHUNK = WIDE
TSTEP = 8
CORR = 0.6
SCALE = (math.log2(math.e) / CORR) ** 2
DECAY = math.log2(math.e) / TSTEP
TINY = 1e-12
RADIANS = math.pi / 180.0
SIDE = 4
PAIR = 2


def rounded(x):
    return x.astype(jnp.bfloat16).astype(jnp.float32)


def split3(x):
    high = rounded(x)
    mid = rounded(x - high)
    return high, mid, rounded(x - high - mid)


def block_kernel(
    prints, times, cells, live, lat_ref, lon_ref, block, payload, own, when, where, alive, lat, lon, cat, rows, pattern, loads_sem, sends_sem
):
    loads = [
        pltpu.make_async_copy(source, target, loads_sem.at[i])
        for i, (source, target) in enumerate(
            ((prints, own), (live, alive), (cells, where), (times, when), (lat_ref, lat), (lon_ref, lon))
        )
    ]
    for load in loads:
        load.start()
    targets = [payload.at[i] for i in range(payload.shape[0])] + [block.at[0]]

    def send(source, start, size, sem):
        copies = [
            pltpu.make_async_copy(source, target.at[pl.ds(start, size), :], sends_sem.at[sem, i])
            for i, target in enumerate(targets)
        ]
        for copy in copies:
            copy.start()
        return copies

    base = lax.axis_index("tm") * TSTEP
    loads[0].wait()
    loads[1].wait()
    for j in range(SLOTS):
        kept = jnp.where(j < alive[0], own[0, j], jnp.zeros((BLOCK, BLOCK), jnp.bfloat16))
        cat[0:BLOCK, j * BLOCK : (j + 1) * BLOCK] = kept
    sends = send(cat.at[pl.ds(0, BLOCK), :], 0, BLOCK, 0)
    for load in loads[2:]:
        load.wait()
    pattern[...] = jnp.zeros_like(pattern)
    pattern[pl.ds(ONE_ROW, 1), :] = jnp.ones((1, WIDE), jnp.float32)
    pattern[pl.ds(LIVE_ROW, 1), :] = jnp.full((1, WIDE), alive[0].astype(jnp.float32))
    for j in range(SLOTS):
        moment = (base + when[0, j]).astype(jnp.float32)
        pattern[pl.ds(TIME_ROW, 1), j * BLOCK : (j + 1) * BLOCK] = jnp.full((1, BLOCK), moment)
        rows[pl.ds(j, 1), :] = lat[pl.ds(where[0, j], 1), :]
        rows[pl.ds(SLOTS + j, 1), :] = lon[pl.ds(where[0, j], 1), :]
    degrees = rows[...].astype(jnp.float32)
    is_lat = lax.broadcasted_iota(jnp.int32, degrees.shape, 0) < SLOTS
    angles = (degrees + jnp.where(is_lat, -89.5, 0.5)) * RADIANS
    cosines, sines = jnp.cos(angles), jnp.sin(angles)
    across = cosines[0:SLOTS]
    units = (across * cosines[SLOTS:], across * sines[SLOTS:], sines[0:SLOTS])
    for c, unit in enumerate(units):
        for part, value in enumerate(split3(unit)):
            for j in range(SLOTS):
                pattern[pl.ds(PARTS * c + part, 1), j * BLOCK : (j + 1) * BLOCK] = value[j : j + 1]
    cat[BLOCK:ROWS, :] = pattern[...].astype(jnp.bfloat16)
    sends += send(cat.at[pl.ds(BLOCK, PATTERN), :], BLOCK, PATTERN, 1)
    for copy in sends:
        copy.wait()


def make_block(footprints, times, cells, live, lat, lon, count):
    hbm = pl.BlockSpec(memory_space=pltpu.HBM)
    return pl.pallas_call(
        block_kernel,
        out_shape=(
            jax.ShapeDtypeStruct((1, ROWS, WIDE), jnp.bfloat16),
            jax.ShapeDtypeStruct((count, ROWS, WIDE), jnp.bfloat16),
        ),
        in_specs=[hbm] * 6,
        out_specs=(hbm, hbm),
        scratch_shapes=[
            pltpu.VMEM((1, SLOTS, BLOCK, BLOCK), jnp.bfloat16),
            pltpu.SMEM((1, SLOTS), jnp.int32),
            pltpu.SMEM((1, SLOTS), jnp.int32),
            pltpu.SMEM((1,), jnp.int32),
            pltpu.VMEM(lat.shape, jnp.int32),
            pltpu.VMEM(lon.shape, jnp.int32),
            pltpu.VMEM((ROWS, WIDE), jnp.bfloat16),
            pltpu.VMEM((2 * SLOTS, BLOCK), jnp.int32),
            pltpu.VMEM((PATTERN, WIDE), jnp.float32),
            pltpu.SemaphoreType.DMA((6,)),
            pltpu.SemaphoreType.DMA((2, count + 1)),
        ],
        compiler_params=pltpu.CompilerParams(vmem_limit_bytes=60 * 2**20),
        name="make_block",
    )(footprints, times, cells, live, lat, lon)


def prepare_near(block, near_rows):
    pattern = block[0, BLOCK:ROWS, :].astype(jnp.float32)
    near_rows[...] = jnp.zeros_like(near_rows)
    for c in range(3):
        high, mid, low = (pattern[PARTS * c + part : PARTS * c + part + 1] for part in range(PARTS))
        scaled = split3((high + mid + low) * (-2.0 * SCALE))
        for segment, value in enumerate(scaled):
            for part in range(PARTS - segment):
                near_rows[pl.ds(segment * PATTERN + PARTS * c + part, 1), :] = value
    ends = split3(jnp.full((1, WIDE), 2.0 * SCALE, jnp.float32))
    for segment, value in enumerate(ends):
        near_rows[pl.ds(segment * PATTERN + ONE_ROW, 1), :] = value
    near_rows[pl.ds(TIME_ROW, 1), :] = jnp.zeros((1, WIDE), jnp.float32)
    return near_rows[...].T.astype(jnp.bfloat16), pattern[TIME_ROW : TIME_ROW + 1]


def weigh(near_vec, near_time, far_pattern, weights, live):
    columns = far_pattern.shape[1]
    far_vec = jnp.concatenate([far_pattern] * PARTS, axis=0)
    far_time = far_pattern.astype(jnp.float32)[TIME_ROW : TIME_ROW + 1]
    for k in range(live):
        rows = pl.ds(k * BLOCK, BLOCK)
        own = jnp.concatenate([near_time[:, k * BLOCK : (k + 1) * BLOCK]] * (columns // BLOCK), axis=1)
        lag = jnp.abs(own - far_time) * (-DECAY)
        square = jnp.maximum(jnp.dot(near_vec[rows, :], far_vec, preferred_element_type=jnp.float32), TINY)
        weights[rows, :] = jnp.exp2(lag - square * lax.rsqrt(square)).astype(jnp.bfloat16)


def local_kernel(*refs):
    *blocks, cov, local, near_rows, near_vec, weights = refs
    last = len(blocks) - 1
    own = blocks[last]
    far_pattern = own[0, BLOCK:ROWS, :]

    def weigh_near(s):
        near_vec[s], when = prepare_near(blocks[s], near_rows)
        weigh(near_vec.at[s], when, far_pattern, weights.at[s % 2], SLOTS)

    def finish(s):
        gain = jnp.dot(blocks[s][0, 0:BLOCK, :], weights[s % 2], preferred_element_type=jnp.float32)
        if s == last:
            for j in range(SLOTS):
                cov[0, j] = gain[:, j * BLOCK : (j + 1) * BLOCK]
        local[s] = lax.dot_general(
            gain.astype(jnp.bfloat16),
            own[0, 0:BLOCK, :],
            (((1,), (1,)), ((), ())),
            preferred_element_type=jnp.float32,
        )

    for s in range(last + 1):
        weigh_near(s)
        if s:
            finish(s - 1)
    finish(last)


def make_local(*blocks):
    vmem = pl.BlockSpec(memory_space=pltpu.VMEM)
    return pl.pallas_call(
        local_kernel,
        out_shape=(
            jax.ShapeDtypeStruct((1, SLOTS, BLOCK, BLOCK), jnp.float32),
            jax.ShapeDtypeStruct((len(blocks), BLOCK, BLOCK), jnp.float32),
        ),
        in_specs=[vmem] * len(blocks),
        out_specs=(vmem, vmem),
        scratch_shapes=[
            pltpu.VMEM((DEPTH, WIDE), jnp.float32),
            pltpu.VMEM((len(blocks), WIDE, DEPTH), jnp.bfloat16),
            pltpu.VMEM((2, WIDE, WIDE), jnp.bfloat16),
        ],
        compiler_params=pltpu.CompilerParams(vmem_limit_bytes=12 * 2**20),
        cost_estimate=pl.CostEstimate(flops=4 * 10**9, bytes_accessed=10**6, transcendentals=2**21),
        name="make_local",
    )(*blocks)


def live_of(pattern):
    count = pattern[:, 0:BLOCK].astype(jnp.float32)[LIVE_ROW : LIVE_ROW + 1]
    return jnp.max(count).astype(jnp.int32)


def columns_at(start, width):
    return pl.ds(pl.multiple_of(start, BLOCK), width)


def tiles_kernel(count, base, placing, *refs):
    blocks, (far, local), refs = refs[:count], refs[count : count + 2], refs[count + 2 :]
    x, odd, earlier = where_placed()
    row = lax.axis_index("obs") // SIDE
    mine = row * PAIR + lax.rem(x - pair_start(x, odd) + SIDE, SIDE)
    known = base >= 0
    if placing:
        before_partner, partner, out, *scratch, wide, wide_partner, own, sems = refs
        outs = (own,)
        wide[...] = before_partner[...].astype(jnp.float32)
        wide_partner[...] = partner[...].astype(jnp.float32)
        copies = spread(wide, out, 0, earlier + PAIR, sems.at[0])
        copies += spread(wide_partner, out, 2 * own.shape[1], pair_start(x, odd) + PAIR, sems.at[1])
        for copy in copies:
            copy.start()
    else:
        outs, scratch = refs[:count], refs[count:]
    near_rows, near_vec, near_time, cats, far_pattern, gain, tiles, weights = scratch
    n_far = far.shape[0]
    near_live = []
    for s in range(count):
        vec, when = prepare_near(blocks[s], near_rows)
        near_vec[s] = vec
        near_time[s] = jnp.broadcast_to(when, near_time.shape[1:])
        cats[s] = blocks[s][0, 0:BLOCK, :]
        near_live.append(live_of(blocks[s][0, BLOCK:ROWS, :]))
    starts, filled = [], jnp.int32(0)
    for r in range(n_far):
        pattern = far[r, BLOCK:ROWS, :]
        far_pattern[:, columns_at(filled * BLOCK, WIDE)] = pattern
        starts.append(filled * BLOCK)
        filled = filled + (jnp.where(r == mine, 0, live_of(pattern)) if known else live_of(pattern))
    far_pattern[:, columns_at(filled * BLOCK, WIDE)] = jnp.zeros((PATTERN, WIDE), jnp.bfloat16)
    chunks = (filled * BLOCK + CHUNK - 1) // CHUNK
    turns = chunks // 2
    gain[:, columns_at(chunks * CHUNK, WIDE)] = jnp.zeros((BLOCK, WIDE), jnp.bfloat16)

    def one_near(s, carry):
        live = near_live[0]
        for other in range(1, count):
            live = jnp.where(s == other, near_live[other], live)

        def weigh_chunk(start, slot, used):
            weigh(
                near_vec.at[s], near_time[s, 0:1, :], far_pattern[:, columns_at(start, CHUNK)], weights.at[slot], used
            )

        def gain_chunk(start, slot, used):
            depth = used * BLOCK
            part = jnp.dot(cats[s, :, 0:depth], weights[slot, 0:depth, :], preferred_element_type=jnp.float32)
            gain[:, columns_at(start, CHUNK)] = part.astype(jnp.bfloat16)

        for used in range(1, SLOTS + 1):

            @pl.when(live == used)
            def _(used=used):
                def turn(i, carry):
                    start = i * 2 * CHUNK
                    weigh_chunk(start, 0, used)
                    gain_chunk(jnp.maximum(start - CHUNK, 0), 1, used)
                    weigh_chunk(start + CHUNK, 1, used)
                    gain_chunk(start, 0, used)
                    return carry

                lax.fori_loop(0, turns, turn, 0)
                rest = turns * 2 * CHUNK

                @pl.when(chunks == 2 * turns)
                def _():
                    gain_chunk(rest - CHUNK, 1, used)

                @pl.when(chunks != 2 * turns)
                def _():
                    weigh_chunk(rest, 0, used)
                    gain_chunk(jnp.maximum(rest - CHUNK, 0), 1, used)
                    gain_chunk(rest, 0, used)

        for r in range(n_far):
            tile = lax.dot_general(
                gain[:, columns_at(starts[r], WIDE)],
                far[r, 0:BLOCK, :],
                (((1,), (1,)), ((), ())),
                preferred_element_type=jnp.float32,
            )
            if known:
                tile = jnp.where(r == mine, local[base + s], tile)
            if count == 1:
                outs[0][:, r * BLOCK : (r + 1) * BLOCK] = tile.astype(outs[0].dtype)
                if placing:
                    last[r].start()
            else:
                tiles[s * n_far + r] = tile.astype(tiles.dtype)
        return carry

    if placing:
        last = spread(own, out, 2 * own.shape[1], pair_start(x, odd), sems.at[2])
    if count == 1:
        one_near(0, 0)
    else:
        lax.fori_loop(0, count, one_near, 0)
        for u in range(count * n_far):
            s, r = u // n_far, u % n_far
            outs[s][:, r * BLOCK : (r + 1) * BLOCK] = tiles[u]
    if placing:
        for copy in copies + last:
            copy.wait()


def make_tiles(blocks, base, far, local, dtype, arrived=()):
    count, n_far = len(blocks), far.shape[0]
    vmem = pl.BlockSpec(memory_space=pltpu.VMEM)
    width = n_far * BLOCK
    scratch = [
        pltpu.VMEM((DEPTH, WIDE), jnp.float32),
        pltpu.VMEM((count, WIDE, DEPTH), jnp.bfloat16),
        pltpu.VMEM((count, 8, WIDE), jnp.float32),
        pltpu.VMEM((count, BLOCK, WIDE), jnp.bfloat16),
        pltpu.VMEM((PATTERN, (n_far + 2) * WIDE), jnp.bfloat16),
        pltpu.VMEM((BLOCK, (n_far + 2) * WIDE), jnp.bfloat16),
        pltpu.VMEM((count * n_far, BLOCK, BLOCK), dtype),
        pltpu.VMEM((2, WIDE, CHUNK), jnp.bfloat16),
    ]
    if arrived:
        out_shape = (jax.ShapeDtypeStruct((BLOCK, 4 * width), jnp.float32),)
        scratch += [pltpu.VMEM((BLOCK, width), jnp.float32)] * 3 + [pltpu.SemaphoreType.DMA((3, SIDE * PAIR))]
        out_specs = (pl.BlockSpec(memory_space=pltpu.HBM),)
    else:
        out_shape = (jax.ShapeDtypeStruct((BLOCK, width), dtype),) * count
        out_specs = (vmem,) * count
    return pl.pallas_call(
        functools.partial(tiles_kernel, count, base, bool(arrived)),
        out_shape=out_shape,
        in_specs=[vmem] * (count + 2 + len(arrived)),
        out_specs=out_specs,
        scratch_shapes=scratch,
        compiler_params=pltpu.CompilerParams(vmem_limit_bytes=16 * 2**20),
        cost_estimate=pl.CostEstimate(
            flops=count * 10**9, bytes_accessed=count * 2 * 10**6, transcendentals=count * 2**22
        ),
        name="make_tiles",
    )(*blocks, far, local, *arrived)


def pair_start(x, odd):
    return jnp.where(odd, lax.rem((x + 3) // PAIR * PAIR + 1, SIDE), x // PAIR * PAIR)


def spread(source, out, base, start, sems):
    copies = []
    for y in range(SIDE):
        for i in range(PAIR):
            column = base + (y * SIDE + lax.rem(start + i, SIDE)) * BLOCK
            u = y * PAIR + i
            copies.append(
                pltpu.make_async_copy(
                    source.at[:, u * BLOCK : (u + 1) * BLOCK], out.at[:, columns_at(column, BLOCK)], sems.at[u]
                )
            )
    return copies


def where_placed():
    x = lax.rem(lax.axis_index("obs"), SIDE)
    odd = lax.rem(lax.axis_index("tm"), 2) == 1
    return x, odd, pair_start(x, jnp.logical_not(odd))


def place_rest_kernel(before, filled, out, wide, sems):
    del filled
    wide[...] = before[...].astype(jnp.float32)
    copies = spread(wide, out, 0, where_placed()[2], sems)
    for copy in copies:
        copy.start()
    for copy in copies:
        copy.wait()


def place_rest(before, filled):
    hbm = pl.BlockSpec(memory_space=pltpu.HBM)
    return pl.pallas_call(
        place_rest_kernel,
        out_shape=jax.ShapeDtypeStruct(filled.shape, filled.dtype),
        in_specs=[pl.BlockSpec(memory_space=pltpu.VMEM), hbm],
        out_specs=hbm,
        input_output_aliases={1: 0},
        scratch_shapes=[pltpu.VMEM(before.shape, jnp.float32), pltpu.SemaphoreType.DMA((SIDE * PAIR,))],
        compiler_params=pltpu.CompilerParams(vmem_limit_bytes=12 * 2**20),
        name="place_rest",
    )(before, filled)


def on_device(footprints, block_times, block_cells, live_counts, cell_lat, cell_lon):
    group = lax.axis_size("obs")
    spans = lax.axis_size("tm")
    axes = ("tm", "obs")
    sides = ((0, 1), (2, 3)), ((1, 2), (3, 0))
    near_by = [
        [t * group + y * SIDE + x for y in range(group // SIDE) for x in pair]
        for t in range(spans)
        for pair in sides[t % 2]
    ]

    def across(t, o):
        x = o % SIDE
        return o - x + (x ^ 1 if t % 2 else SIDE - 1 - x)

    def steps(by, crossing):
        pairs = []
        for t in range(spans):
            if 0 <= t + by < spans:
                for o in range(group):
                    other = across(min(t, t + by), o) if crossing else o
                    pairs.append((t * group + o, (t + by) * group + other))
        return pairs

    lat = cell_lat.reshape(-1, BLOCK)
    lon = cell_lon.reshape(-1, BLOCK)
    block, payload = make_block(
        footprints, block_times, block_cells, live_counts, lat, lon, group // (SIDE // PAIR)
    )
    far = lax.all_to_all(payload, axes, 0, 0, tiled=True, axis_index_groups=near_by)
    partner_block = lax.ppermute(block, axes, steps(0, True))
    next_block = lax.ppermute(block, axes, steps(-1, False))
    next_partner_block = lax.ppermute(block, axes, steps(-1, True))
    footprint_cov, local = make_local(partner_block, next_partner_block, block)
    far, local = lax.optimization_barrier((far, local))
    (next_partner_tiles,) = make_tiles((next_partner_block,), 1, far, local, jnp.bfloat16)
    before_partner = lax.ppermute(next_partner_tiles, axes, steps(1, True))
    far, next_partner_tiles = lax.optimization_barrier((far, next_partner_tiles))
    (partner_tiles,) = make_tiles((partner_block,), 0, far, local, jnp.bfloat16)
    partner = lax.ppermute(partner_tiles, axes, steps(0, True))
    far, partner_tiles = lax.optimization_barrier((far, partner_tiles))
    (next_tiles,) = make_tiles((next_block,), -1, far, local, jnp.bfloat16)
    before = lax.ppermute(next_tiles, axes, steps(1, False))
    (filled,) = make_tiles((block,), 2, far, local, jnp.float32, (before_partner, partner))
    cross_cov = place_rest(before, filled)
    return (cross_cov, footprint_cov)


def solution(mesh):
    placed = (
        P(("tm", "obs"), None, None, None),
        P(("tm", "obs"), None),
        P(("tm", "obs"), None),
        P(("tm", "obs")),
        P(),
        P(),
    )
    return jax.shard_map(
        on_device,
        mesh=mesh,
        in_specs=placed,
        out_specs=(P(("tm", "obs"), None), P(("tm", "obs"), None, None, None)),
        check_vma=False,
    )
```
